128 devices in a mesh: fsdp: 8 (over x, z_hi), tp: 16 (over y, z_lo, core).
Axes of the slice: x: 4, y: 4, z: 4 (z_hi: 2, z_lo: 2; z = z_hi * 2 + z_lo), core: 2. Of those that a mesh axis runs over, the one named last changes fastest.
Arguments:
- hidden_in: bfloat16 [4096, 8192], P('fsdp'), may hold values from -100 to 100
- lengths: int32 [8, 8], P('fsdp'), may hold values from 1 to 256, 512 in all within a row
- norm_gain: float32 [8192], replicated, may hold values from 0.5 to 4
- query_weight: bfloat16 [8192, 8192], P(('fsdp', 'tp')), may hold values from -0.088388348 to 0.088388348
- key_weight: bfloat16 [8192, 1024], P(('fsdp', 'tp')), may hold values from -0.088388348 to 0.088388348
- value_weight: bfloat16 [8192, 1024], P(('fsdp', 'tp')), may hold values from -0.0625 to 0.0625
- out_weight: bfloat16 [8192, 8192], P(None, ('fsdp', 'tp')), may hold values from -0.0625 to 0.0625
- query_scale: float32 [8192], replicated, may hold values from 2.2097087e-05 to 0.00022097086
- key_scale: float32 [1024], replicated, may hold values from 2.2097087e-05 to 0.00022097086
- value_scale: float32 [1024], replicated, may hold values from 2.2097087e-05 to 0.00022097086
- out_scale: float32 [8192], replicated, may hold values from 2.2097087e-05 to 0.00022097086
Outputs:
- layer_out: bfloat16 [4096, 8192], P(('fsdp', 'tp'))
The draws below stay inside these ranges and needn't reach their ends.
Inputs may be any that keep to these rules, and one draw needn't show every extreme that they name: `lengths`: each row sums to 512, and its largest entry is exactly 256.
All inputs are finite; a program needn't handle non-finite values.
Results may differ from the reference program's by a relative error of at most 0.024.
Values may be sent and summed in bfloat16 or wider, within the bound.
A program may use at most 128 MiB of HBM per device.

```python
import math
import jax
import jax.numpy as jnp
import numpy as np
from jax import lax

D = 8192
H = 64
KV = 8
HD = 128
TOK = 512
DOCS = 8
REPLICAS = 8
ROWS = 4096
N_TP = 16


def draw_hidden_in(key, part):
    key = jax.random.fold_in(key, 11)
    key_base, key_rows, key_cols = jax.random.split(key, 3)
    row_factor = jnp.exp(jax.random.uniform(key_rows, (ROWS, 1), jnp.float32, 0.0, math.log(10.0)))
    col_factor = jnp.exp(jax.random.uniform(key_cols, (1, D), jnp.float32, math.log(0.5), math.log(2.0)))
    base = jnp.clip(jax.random.normal(key_base, (ROWS, D), jnp.float32), -5.0, 5.0)
    result = base * row_factor * col_factor
    return result.astype(jnp.bfloat16)


def draw_norm_gain(key, part):
    key = jax.random.fold_in(key, 23)
    spread = jax.random.uniform(key, (D,), jnp.float32, math.log(0.5), math.log(2.0))
    return jnp.exp(spread).astype(jnp.float32)


def draw_query_weight(key, part):
    key = jax.random.fold_in(key, 31)
    base = jnp.clip(jax.random.normal(key, (D, H * HD), jnp.float32), -6.0, 6.0) * D ** (-0.5)
    return base.astype(jnp.bfloat16)


def draw_key_weight(key, part):
    key = jax.random.fold_in(key, 37)
    base = jnp.clip(jax.random.normal(key, (D, KV * HD), jnp.float32), -6.0, 6.0) * D ** (-0.5)
    return base.astype(jnp.bfloat16)


def level_of(key, shape, cuts, least, top_value):
    level, own = 1.0, jax.random.fold_in(key, 6)
    for dim, shards_of in cuts:
        steps = jnp.exp(jax.random.uniform(jax.random.fold_in(own, dim), (shards_of,), jnp.float32, least / len(cuts), top_value / len(cuts)))
        level = level * jnp.repeat(steps, shape[dim] // shards_of).reshape([-1 if axis == dim else 1 for axis in range(len(shape))])
    return level


def length_profile(amount, total, limit, skew):
    weights = [(1 << 20) // math.isqrt(grade ** skew) + 1 for grade in range(2, amount + 1)]
    rest, counts = total - limit - (amount - 1), [1] * (amount - 1)
    while rest > 0:
        free = [i for i in range(amount - 1) if counts[i] < limit]
        mass, remaining = sum([weights[i] for i in free]), rest
        for i in free:
            more = min(limit - counts[i], max(1, remaining * weights[i] // mass), rest)
            counts[i] = counts[i] + more
            rest = rest - more
    return np.array([limit] + counts)


def ragged(rng, number_of, total, limit, lean):
    if number_of == 2:
        one = jax.random.randint(rng, (), max(1, total - limit), min(limit, total - 1) + 1)
        return jnp.stack([one, total - one])
    sizes = jnp.asarray(length_profile(number_of, total, limit, lean), jnp.int32)
    pairs = (number_of - 1) // 2
    donor, sink = sizes[1:1 + 2 * pairs:2], sizes[2:2 + 2 * pairs:2]
    room = jnp.minimum(donor - 1, limit - sink)
    passed = jax.random.randint(jax.random.fold_in(rng, 1), (pairs,), 0, 1 << 20) % (room + 1)
    sizes = sizes.at[1:1 + 2 * pairs:2].set(donor - passed).at[2:2 + 2 * pairs:2].set(sink + passed)
    return sizes[jax.random.permutation(jax.random.fold_in(rng, 2), number_of)]


def bell_draw(stream_key, shape, scale, bound, pieces=(), kind=jnp.bfloat16):
    entries = jax.random.normal(stream_key, shape, jnp.float32) * scale
    if len(pieces) > 0:
        entries = level_of(stream_key, shape, pieces, -0.22, 0.18) * entries
    return jnp.clip(entries, min=-bound, max=bound).astype(kind)


def setup_inputs(seed: int = 0) -> dict:
    key_of = jax.random.split(jax.random.key(seed), 12)
    hidden_in = draw_hidden_in(jax.random.fold_in(key_of[11], 71), 0)
    lengths = jax.vmap(lambda own: ragged(own, DOCS, TOK, TOK // 2, 2))(jax.random.split(key_of[1], REPLICAS)).reshape((REPLICAS, DOCS)).astype(jnp.int32)
    norm_gain = draw_norm_gain(jax.random.fold_in(key_of[11], 71), 0)
    query_weight = draw_query_weight(jax.random.fold_in(key_of[11], 71), 0)
    key_weight = draw_key_weight(jax.random.fold_in(key_of[11], 71), 0)
    value_weight = bell_draw(key_of[5], (D, KV * HD), D ** -0.5, 0.0625, ((0, 128),))
    out_weight = bell_draw(key_of[6], (H * HD, D), (H * HD) ** -0.5, 0.0625, ((1, 128),))
    query_scale = jnp.clip(jnp.exp(jax.random.uniform(key_of[7], (H * HD,), jnp.float32, math.log(2.209708691225387e-05), math.log(0.00022097086))), 2.209708691225387e-05, 0.00022097086)
    key_scale = jnp.clip(jnp.exp(jax.random.uniform(key_of[8], (KV * HD,), jnp.float32, math.log(2.209708691225387e-05), math.log(0.00022097086))), 2.209708691225387e-05, 0.00022097086)
    value_scale = jnp.clip(jnp.exp(jax.random.uniform(key_of[9], (KV * HD,), jnp.float32, math.log(2.209708691225387e-05), math.log(0.00022097086))), 2.209708691225387e-05, 0.00022097086)
    out_scale = jnp.clip(jnp.exp(jax.random.uniform(key_of[10], (D,), jnp.float32, math.log(2.209708691225387e-05), math.log(0.00022097086))), 2.209708691225387e-05, 0.00022097086)
    return dict(hidden_in=hidden_in, lengths=lengths, norm_gain=norm_gain, query_weight=query_weight, key_weight=key_weight, value_weight=value_weight, out_weight=out_weight, query_scale=query_scale, key_scale=key_scale, value_scale=value_scale, out_scale=out_scale)


SATURATE = 448.0
EPSILON = 1e-06
ROPE_BASE = 1000000.0
MASKED_SCORE = -1e+30

def quantize(weight, scale):
    scaled = weight.astype(jnp.float32) / scale.astype(jnp.float32)
    return jnp.clip(scaled, -SATURATE, SATURATE).astype(jnp.bfloat16)

def documents(lengths, window):
    doc_ends = jnp.cumsum(lengths).astype(jnp.int32)
    doc_starts = (doc_ends - lengths).astype(jnp.int32)
    places = jnp.arange(window, dtype=jnp.int32)
    doc_ids = lax.optimization_barrier(jnp.sum((places[:, None] >= doc_ends[None, :]).astype(jnp.int32), axis=1)).astype(jnp.int32)
    labels = jnp.arange(lengths.shape[0], dtype=jnp.int32)
    doc_begin = lax.optimization_barrier(jnp.sum(jnp.where(doc_ids[:, None] == labels[None, :], doc_starts[None, :], 0), axis=1)).astype(jnp.int32)
    return (doc_ids, (places - doc_begin).astype(jnp.int32))

def rope_tables(position, head_dim):
    half_dim = head_dim // 2
    frequency = jnp.exp(jnp.arange(half_dim, dtype=jnp.float32) * (-2.0 * math.log(ROPE_BASE) / head_dim))
    angles = position.astype(jnp.float32)[:, None] * frequency[None, :]
    return (jnp.cos(angles), jnp.sin(angles))

def rotate(vectors, cosine_table, sine_table):
    half_dim = vectors.shape[-1] // 2
    front_half = vectors[..., :half_dim]
    back_half = vectors[..., half_dim:]
    cos_part = cosine_table[:, None, :]
    sin_part = sine_table[:, None, :]
    return jnp.concatenate([front_half * cos_part - back_half * sin_part, back_half * cos_part + front_half * sin_part], axis=-1)

def replica(rows_in, lengths, norm_gain, query_stored, key_stored, value_stored, out_stored, query_scale, key_scale, value_scale, out_scale):
    widened = rows_in.astype(jnp.float32)
    inv_rms = lax.rsqrt(lax.optimization_barrier(jnp.mean(widened * widened, axis=1, keepdims=True)) + EPSILON)
    normed = (widened * inv_rms * norm_gain).astype(jnp.bfloat16)
    doc_ids, position = documents(lengths, TOK)
    cosine_table, sine_table = rope_tables(position, HD)
    query_proj = jnp.dot(normed, query_stored, preferred_element_type=jnp.float32) * query_scale
    queries = rotate(query_proj.reshape(TOK, H, HD), cosine_table, sine_table).astype(jnp.bfloat16)
    key_raw = (jnp.dot(normed, key_stored, preferred_element_type=jnp.float32) * key_scale).astype(jnp.bfloat16)
    key_raw = lax.optimization_barrier(key_raw)
    key_rot = rotate(key_raw.astype(jnp.float32).reshape(TOK, KV, HD), cosine_table, sine_table).astype(jnp.bfloat16)
    values = (jnp.dot(normed, value_stored, preferred_element_type=jnp.float32) * value_scale).astype(jnp.bfloat16)
    values = values.reshape(TOK, KV, HD)
    places = jnp.arange(TOK, dtype=jnp.int32)
    allowed = (doc_ids[:, None] == doc_ids[None, :]) & (places[None, :] <= places[:, None])
    group_size = H // KV

    def one_head(head_idx):
        query_head = lax.dynamic_index_in_dim(queries, head_idx, 1, keepdims=False)
        key_head = lax.dynamic_index_in_dim(key_rot, head_idx // group_size, 1, keepdims=False)
        value_head = lax.dynamic_index_in_dim(values, head_idx // group_size, 1, keepdims=False)
        scores = jnp.dot(query_head, key_head.T, preferred_element_type=jnp.float32) * HD ** (-0.5)
        scores = jnp.where(allowed, scores, MASKED_SCORE)
        row_max = lax.optimization_barrier(jnp.max(scores, axis=1, keepdims=True))
        weights = jnp.exp(scores - row_max)
        probabilities = (weights / lax.optimization_barrier(jnp.sum(weights, axis=1, keepdims=True))).astype(jnp.bfloat16)
        return jnp.dot(probabilities, value_head, preferred_element_type=jnp.float32).astype(jnp.bfloat16)
    head_outs = lax.map(one_head, jnp.arange(H, dtype=jnp.int32))
    attended = jnp.transpose(head_outs, (1, 0, 2)).reshape(TOK, H * HD)
    group_width = H * HD // N_TP

    def add_group(group_idx, running):
        start_col = (group_idx * group_width).astype(jnp.int32)
        col_block = lax.dynamic_slice_in_dim(attended, start_col, group_width, 1)
        row_block = lax.dynamic_slice_in_dim(out_stored, start_col, group_width, 0)
        partial_value = jnp.dot(col_block, row_block, preferred_element_type=jnp.float32).astype(jnp.bfloat16)
        partial_value = lax.optimization_barrier(partial_value)
        return running + partial_value.astype(jnp.float32)
    running = lax.fori_loop(0, N_TP, add_group, jnp.zeros((TOK, D), jnp.float32))
    return (running * out_scale).astype(jnp.bfloat16)

def reference(hidden_in, lengths, norm_gain, query_weight, key_weight, value_weight, out_weight, query_scale, key_scale, value_scale, out_scale):
    query_stored = quantize(query_weight, query_scale)
    key_stored = quantize(key_weight, key_scale)
    value_stored = quantize(value_weight, value_scale)
    out_stored = quantize(out_weight, out_scale)
    blocks = hidden_in.reshape(REPLICAS, TOK, D)

    def per_replica(replica_in):
        return replica(replica_in[0], replica_in[1], norm_gain, query_stored, key_stored, value_stored, out_stored, query_scale, key_scale, value_scale, out_scale)
    layer_out = lax.map(per_replica, (blocks, lengths))
    return layer_out.reshape(ROWS, D)
```

```python
import math

import jax
import jax.numpy as jnp
from jax import lax
from jax.experimental import pallas as pl
from jax.experimental.pallas import tpu as pltpu
from jax.sharding import PartitionSpec as P

MESH = pl.DeviceIdType.MESH
F32 = jnp.float32
BF16 = jnp.bfloat16

HD = 128
TOK = 512
D = 8192
SATURATE = 448.0
EPSILON = 1e-06
ROPE_BASE = 1000000.0
MASKED_SCORE = -1e30

TREE = {
    (1, 0): (0, 0, 1),
    (3, 0): (0, 0, -1),
    (0, 1): (0, 0, 0),
    (2, 0): (1, 0, 1),
    (2, 1): (2, 0, 0),
    (1, 1): (0, 1, 1),
    (3, 1): (0, 1, -1),
}


class Gather:
    def __init__(self, slot, piece, send_sem, recv_sem, plus, minus, pair):
        self.slot, self.piece = slot, piece
        self.send_sem, self.recv_sem = send_sem, recv_sem
        self.to = {1: plus, -1: minus, 0: pair}

    def index(self, u, dz, h):
        return self.slot(u if h == 0 else (4 - u) % 4, dz)

    def copy(self, u, dz, h):
        su, sdz, step = TREE[(u, dz)]
        ref = self.piece(self.index(su, sdz, h), h)
        return pltpu.make_async_remote_copy(
            src_ref=ref,
            dst_ref=ref,
            send_sem=self.send_sem.at[h, u * 2 + dz],
            recv_sem=self.recv_sem.at[h, u * 2 + dz],
            device_id=self.to[step if h == 0 else -step],
            device_id_type=MESH,
        )

    def send(self, h, *targets):
        for u, dz in targets:
            self.copy(u, dz, h).start()

    def arrived(self, u, dz, h):
        ref = self.piece(self.index(u, dz, h), h)
        pltpu.make_async_remote_copy(
            src_ref=ref,
            dst_ref=ref,
            send_sem=self.send_sem.at[h, u * 2 + dz],
            recv_sem=self.recv_sem.at[h, u * 2 + dz],
            device_id=self.to[0],
            device_id_type=MESH,
        ).wait_recv()

    def sent(self):
        for h in range(2):
            for u, dz in TREE:
                self.copy(u, dz, h).wait_send()


def choose(i, values):
    result = values[-1]
    for n in range(len(values) - 2, -1, -1):
        result = jnp.where(i == n, values[n], result)
    return result


def kernel(
    hidden_ref, lengths_ref, gain_ref, wq_ref, wk_ref, wv_ref, wo_ref, qs_ref, ks_ref, vs_ref, os_ref,
    out_ref,
    nrm, raw_q, raw_k, raw_v, raw_o, snd, wqkv, wo, ww_own, ww_snd, ww_got, acc, cos_t, sin_t, begin_t,
    q_t, kv_t, att, acc_o, ost, got,
    load_sem, a2a_s, a2a_r, core_s, core_r, q_s, q_r, o_s, o_r, att_s, att_r, fin_s, fin_r,
):
    f = lax.axis_index("fsdp")
    t = lax.axis_index("tp")
    x, zh = f // 2, f % 2
    y, zl, c = t // 4, (t // 2) % 2, t % 2
    rz = (zl + zh) % 2
    role = y * 2 + rz
    hb = role * 2 + c

    def device(ff, tt):
        return {"fsdp": ff, "tp": tt}

    x_plus = device(((x + 1) % 4) * 2 + zh, t)
    x_minus = device(((x + 3) % 4) * 2 + zh, t)
    z_pair = device(x * 2 + 1 - zh, y * 4 + (1 - zl) * 2 + c)
    y_plus = device(f, ((y + 1) % 4) * 4 + zl * 2 + c)
    y_minus = device(f, ((y + 3) % 4) * 4 + zl * 2 + c)
    zl_pair = device(f, y * 4 + (1 - zl) * 2 + c)
    core_pair = device(f, y * 4 + zl * 2 + 1 - c)

    barrier = pltpu.get_barrier_semaphore()
    for other in (x_plus, x_minus, z_pair):
        pl.semaphore_signal(barrier, inc=1, device_id=other, device_id_type=MESH)

    @pl.loop(1, 16)
    def _(i):
        pl.semaphore_signal(barrier, inc=1, device_id=device(f, (t + i) % 16), device_id_type=MESH)

    loads = [
        pltpu.make_async_copy(src, dst, load_sem.at[n])
        for n, (src, dst) in enumerate(
            [(wq_ref, raw_q), (wk_ref, raw_k), (wv_ref, raw_v), (wo_ref, raw_o), (hidden_ref, nrm)]
        )
    ]
    for load in loads:
        load.start()

    def quantize(weight, inverse):
        return jnp.clip(weight.astype(F32) * inverse, -SATURATE, SATURATE).astype(BF16)

    for load in loads[:3]:
        load.wait()

    @pl.loop(0, 8)
    def _(r):
        for n in range(2):
            cols = pl.ds(pl.multiple_of((r * 2 + n) * 512, 512), 512)
            snd[r * 2 + n, :, 0:512] = quantize(raw_q[:, cols], 1.0 / qs_ref[:, cols])
        cols = pl.ds(pl.multiple_of(r * 128, 128), 128)
        snd[r * 2, :, 512:640] = quantize(raw_k[:, cols], 1.0 / ks_ref[:, cols])
        snd[r * 2 + 1, :, 512:640] = quantize(raw_v[:, cols], 1.0 / vs_ref[:, cols])

    pl.semaphore_wait(barrier, 18)

    def block_copy(i):
        to = (t + i) % 16
        block = ((to // 4) * 2 + ((to // 2) % 2 + zh) % 2) * 2 + to % 2
        return pltpu.make_async_remote_copy(
            src_ref=snd.at[block],
            dst_ref=wqkv.at[f, pl.ds(pl.multiple_of(t * 64, 64), 64)],
            send_sem=a2a_s.at[i],
            recv_sem=a2a_r.at[i],
            device_id=device(f, to),
            device_id_type=MESH,
        )

    @pl.loop(1, 16)
    def _(i):
        block_copy(i).start()

    wqkv[f, pl.ds(pl.multiple_of(t * 64, 64), 64)] = snd[hb]

    loads[3].wait()
    chip_cols = pl.ds(pl.multiple_of((f * 8 + t // 2) * 128, 128), 128)
    chip_scale = 1.0 / os_ref[:, chip_cols]
    own_scale = jnp.where(c == 0, chip_scale[:, :64], chip_scale[:, 64:])

    def twice(block):
        part = quantize(raw_o[pl.ds(pl.multiple_of(block * 512, 512), 512), :], own_scale)
        return jnp.concatenate([part, part], axis=1)

    @pl.loop(0, 8)
    def _(r):
        ww_snd[pl.ds(pl.multiple_of(r * 512, 512), 512)] = twice(r * 2 + 1 - c)

    core_w = pltpu.make_async_remote_copy(
        src_ref=ww_snd, dst_ref=ww_got, send_sem=core_s.at[0], recv_sem=core_r.at[0],
        device_id=core_pair, device_id_type=MESH,
    )
    core_w.start()

    @pl.loop(0, 8)
    def _(r):
        ww_own[pl.ds(pl.multiple_of(r * 512, 512), 512)] = twice(r * 2 + c)

    core_w.wait_recv()

    @pl.loop(0, 8)
    def _(r):
        rows = pl.ds(pl.multiple_of(r * 512, 512), 512)
        lane = lax.broadcasted_iota(jnp.int32, (512, 128), 1)
        mine = (lane // 64) == c
        wo[f, rows] = jnp.where(mine, ww_own[rows].astype(F32), ww_got[rows].astype(F32)).astype(BF16)

    def fsdp_slot(dx, dz):
        return ((x + 4 - dx) % 4) * 2 + (zh + dz) % 2

    out_gather = Gather(
        fsdp_slot, lambda s, h: wo.at[s, pl.ds(h * 2048, 2048)], o_s, o_r, x_plus, x_minus, z_pair
    )
    in_gather = Gather(
        fsdp_slot, lambda s, h: wqkv.at[s, pl.ds(h * 512, 512)], q_s, q_r, x_plus, x_minus, z_pair
    )
    att_gather = Gather(
        lambda dy, dz: ((y + 4 - dy) % 4) * 2 + (rz + dz) % 2,
        lambda s, h: att.at[s, h], att_s, att_r, y_plus, y_minus, zl_pair,
    )
    for h in range(2):
        out_gather.send(h, (1, 0), (3, 0), (0, 1))

    loads[4].wait()

    @pl.loop(0, 32)
    def _(i):
        rows = pl.ds(pl.multiple_of(i * 16, 16), 16)
        wide = nrm[rows, :].astype(F32)
        inverse = lax.rsqrt(jnp.mean(wide * wide, axis=1, keepdims=True) + EPSILON)
        nrm[rows, :] = (wide * inverse * gain_ref[...]).astype(BF16)

    place = lax.broadcasted_iota(jnp.int32, (TOK, 128), 0)
    begin = jnp.zeros((TOK, 128), jnp.int32)
    start = lengths_ref[0, 0]
    for n in range(1, 8):
        begin = jnp.where(place >= start, start, begin)
        start = start + lengths_ref[0, n]
    begin_t[...] = begin
    lane = lax.broadcasted_iota(jnp.int32, (TOK, 128), 1)
    frequency = jnp.exp((lane % 64).astype(F32) * (-2.0 * math.log(ROPE_BASE) / HD))
    angle = (place - begin).astype(F32) * frequency
    cos_t[...] = jnp.cos(angle)
    sine = jnp.sin(angle)
    sin_t[...] = jnp.where(lane < 64, -sine, sine)

    for h in range(2):
        @pl.loop(h * 8, h * 8 + 8)
        def _(src):
            @pl.when(src != t)
            def _():
                ref = wqkv.at[f, pl.ds(pl.multiple_of(src * 64, 64), 64)]
                i = (t + 16 - src) % 16
                pltpu.make_async_remote_copy(
                    src_ref=ref, dst_ref=ref, send_sem=a2a_s.at[i], recv_sem=a2a_r.at[i],
                    device_id=core_pair, device_id_type=MESH,
                ).wait_recv()

        in_gather.send(h, (1, 0), (3, 0), (0, 1))

    acc[...] = jnp.zeros_like(acc)

    def project(*pieces):
        slots = [in_gather.index(u, dz, h) for u, dz, h in pieces]
        halves = [h for _, _, h in pieces]

        @pl.loop(0, len(pieces))
        def _(i):
            s, h = choose(i, slots), choose(i, halves)
            cols = pl.ds(pl.multiple_of(s * 1024 + h * 512, 512), 512)
            acc[...] += jnp.dot(
                nrm[:, cols], wqkv[s, pl.ds(pl.multiple_of(h * 512, 512), 512), :], preferred_element_type=F32
            )

    project((0, 0, 0), (0, 0, 1))
    for h in range(2):
        in_gather.arrived(1, 0, h)
        in_gather.send(h, (2, 0))
    in_gather.arrived(0, 1, 0)
    in_gather.send(0, (1, 1), (3, 1))
    project((1, 0, 0), (1, 0, 1), (0, 1, 0))
    for h in range(2):
        in_gather.arrived(3, 0, h)
    in_gather.arrived(0, 1, 1)
    in_gather.send(1, (1, 1), (3, 1))
    project((3, 0, 0), (3, 0, 1), (0, 1, 1))
    for h in range(2):
        in_gather.arrived(2, 0, h)
        in_gather.send(h, (2, 1))
    project((2, 0, 0), (2, 0, 1))
    in_gather.arrived(1, 1, 0)
    in_gather.arrived(1, 1, 1)
    for h in range(2):
        out_gather.arrived(1, 0, h)
        out_gather.send(h, (2, 0))
    in_gather.arrived(2, 1, 0)
    project((1, 1, 0), (1, 1, 1), (2, 1, 0))
    in_gather.arrived(3, 1, 0)
    in_gather.arrived(3, 1, 1)
    for h in range(2):
        out_gather.arrived(0, 1, h)
        out_gather.send(h, (1, 1), (3, 1))
    in_gather.arrived(2, 1, 1)
    project((3, 1, 0), (3, 1, 1), (2, 1, 1))

    def rope(v):
        return v * cos_t[...] + pltpu.roll(v, 64, axis=1) * sin_t[...]

    kv_cols = pl.ds(pl.multiple_of(role * 128, 128), 128)
    key_raw = (acc[:, 512:640] * ks_ref[:, kv_cols]).astype(BF16).astype(F32)
    value = acc[:, 512:640] * vs_ref[:, kv_cols]
    kv_t[c] = jnp.where(c == 0, rope(key_raw), value).astype(BF16)
    core_kv = pltpu.make_async_remote_copy(
        src_ref=kv_t.at[c], dst_ref=kv_t.at[c], send_sem=core_s.at[1], recv_sem=core_r.at[1],
        device_id=core_pair, device_id_type=MESH,
    )
    core_kv.start()

    @pl.loop(0, 4)
    def _(n):
        cols = pl.ds(pl.multiple_of(n * 128, 128), 128)
        scale = qs_ref[:, pl.ds(pl.multiple_of(hb * 512 + n * 128, 128), 128)]
        q_t[n] = rope(acc[:, cols] * scale).astype(BF16)

    other = kv_t.at[1 - c]
    pltpu.make_async_remote_copy(
        src_ref=other, dst_ref=other, send_sem=core_s.at[1], recv_sem=core_r.at[1],
        device_id=core_pair, device_id_type=MESH,
    ).wait_recv()

    for h in range(2):
        for n in range(2):
            for b in range(4):
                first = max(0, b * 128 - 256)
                width = (b + 1) * 128 - first
                rows = slice(b * 128, (b + 1) * 128)
                keys = slice(first, first + width)
                scores = lax.dot_general(
                    q_t[h * 2 + n, rows], kv_t[0, keys], (((1,), (1,)), ((), ())), preferred_element_type=F32
                ) * HD ** (-0.5)
                p = lax.broadcasted_iota(jnp.int32, (128, width), 0) + b * 128
                s = lax.broadcasted_iota(jnp.int32, (128, width), 1) + first
                keep = (s <= p) & (s >= begin_t[rows, 0:1])
                scores = jnp.where(keep, scores, MASKED_SCORE)
                weights = jnp.exp(scores - jnp.max(scores, axis=1, keepdims=True))
                total = jnp.sum(weights, axis=1, keepdims=True)
                mixed = jnp.dot(weights.astype(BF16), kv_t[1, keys], preferred_element_type=F32)
                att[role, h, rows, n * 128:(n + 1) * 128] = (mixed / total).astype(BF16)
        att_gather.send(h, (1, 0), (3, 0), (0, 1))

    early = [fsdp_slot(dx, dz) for dx, dz in ((0, 0), (1, 0), (3, 0), (0, 1))]
    late = [fsdp_slot(dx, dz) for dx, dz in ((2, 0), (1, 1), (3, 1), (2, 1))]

    def mix(which, slots, pieces):
        roles = [att_gather.index(u, dz, h) for u, dz, h in pieces]
        halves = [h for _, _, h in pieces]

        @pl.loop(0, len(pieces))
        def _(i):
            r, h = choose(i, roles), choose(i, halves)
            rows = pl.ds(pl.multiple_of(r * 512 + h * 256, 256), 256)
            columns = jnp.concatenate([wo[s, rows] for s in slots], axis=1)
            acc_o[which] += jnp.dot(att[r, h], columns, preferred_element_type=F32)

    def finish(which):
        ost[which] = acc_o[which].astype(BF16)

        @pl.loop(1, 16)
        def _(i):
            final_copy(which, i).start()

        got[which, t] = ost[which, pl.ds(pl.multiple_of(t * 32, 32), 32)]

    def final_copy(which, i):
        to = (t + i) % 16
        return pltpu.make_async_remote_copy(
            src_ref=ost.at[which, pl.ds(pl.multiple_of(to * 32, 32), 32)],
            dst_ref=got.at[which, t],
            send_sem=fin_s.at[which, i],
            recv_sem=fin_r.at[which, i],
            device_id=device(f, to),
            device_id_type=MESH,
        )

    acc_o[...] = jnp.zeros_like(acc_o)
    for h in range(2):
        out_gather.arrived(3, 0, h)
    mix(0, early, [(0, 0, 0), (0, 0, 1)])
    for h in range(2):
        att_gather.arrived(1, 0, h)
        att_gather.send(h, (2, 0))
        att_gather.arrived(0, 1, h)
        att_gather.send(h, (1, 1), (3, 1))
    mix(0, early, [(1, 0, 0), (1, 0, 1), (0, 1, 0), (0, 1, 1)])
    for h in range(2):
        out_gather.arrived(2, 0, h)
        out_gather.send(h, (2, 1))
    for h in range(2):
        att_gather.arrived(3, 0, h)
    for h in range(2):
        att_gather.arrived(2, 0, h)
        att_gather.send(h, (2, 1))
    mix(0, early, [(3, 0, 0), (3, 0, 1), (2, 0, 0), (2, 0, 1)])
    for h in range(2):
        for u in (1, 3, 2):
            att_gather.arrived(u, 1, h)
    mix(0, early, [(u, 1, h) for u in (1, 3, 2) for h in range(2)])
    finish(0)
    for h in range(2):
        for u in (1, 3, 2):
            out_gather.arrived(u, 1, h)
    mix(1, late, [(u, dz, h) for u in range(4) for dz in range(2) for h in range(2)])
    finish(1)

    def collect(which, offsets):
        @pl.loop(1, 16)
        def _(i):
            ref = got.at[which, (t + 16 - i) % 16]
            pltpu.make_async_remote_copy(
                src_ref=ref, dst_ref=ref, send_sem=fin_s.at[which, i], recv_sem=fin_r.at[which, i],
                device_id=core_pair, device_id_type=MESH,
            ).wait_recv()

        @pl.loop(0, 8)
        def _(k):
            for n, (dx, dz) in enumerate(offsets):
                chip = (k // 2) * 2 + (k % 2 + dz) % 2
                cols = pl.ds(pl.multiple_of((fsdp_slot(dx, dz) * 8 + chip) * 128, 128), 128)
                part = slice(n * 128, (n + 1) * 128)
                both = got[which, k * 2, :, part].astype(F32) + got[which, k * 2 + 1, :, part].astype(F32)
                out_ref[:, cols] = (both * os_ref[:, cols]).astype(BF16)

    collect(0, ((0, 0), (1, 0), (3, 0), (0, 1)))
    collect(1, ((2, 0), (1, 1), (3, 1), (2, 1)))

    @pl.loop(1, 16)
    def _(i):
        block_copy(i).wait_send()
        final_copy(0, i).wait_send()
        final_copy(1, i).wait_send()

    core_w.wait_send()
    core_kv.wait_send()
    out_gather.sent()
    in_gather.sent()
    att_gather.sent()


def shards(
    hidden_in, lengths, norm_gain, query_weight, key_weight, value_weight, out_weight,
    query_scale, key_scale, value_scale, out_scale,
):
    vmem = pl.BlockSpec(memory_space=pltpu.VMEM)
    any_space = pl.BlockSpec(memory_space=pl.ANY)
    smem = pl.BlockSpec(memory_space=pltpu.SMEM)
    dma = pltpu.SemaphoreType.DMA
    return pl.pallas_call(
        kernel,
        out_shape=jax.ShapeDtypeStruct((32, D), BF16),
        in_specs=[any_space, smem, vmem, any_space, any_space, any_space, any_space, vmem, vmem, vmem, vmem],
        out_specs=vmem,
        scratch_shapes=[
            pltpu.VMEM((TOK, D), BF16),
            pltpu.VMEM((64, D), BF16),
            pltpu.VMEM((64, 1024), BF16),
            pltpu.VMEM((64, 1024), BF16),
            pltpu.VMEM((D, 64), BF16),
            pltpu.VMEM((16, 64, 640), BF16),
            pltpu.VMEM((8, 1024, 640), BF16),
            pltpu.VMEM((8, 4096, 128), BF16),
            pltpu.VMEM((4096, 128), BF16),
            pltpu.VMEM((4096, 128), BF16),
            pltpu.VMEM((4096, 128), BF16),
            pltpu.VMEM((TOK, 640), F32),
            pltpu.VMEM((TOK, HD), F32),
            pltpu.VMEM((TOK, HD), F32),
            pltpu.VMEM((TOK, HD), jnp.int32),
            pltpu.VMEM((4, TOK, HD), BF16),
            pltpu.VMEM((2, TOK, HD), BF16),
            pltpu.VMEM((8, 2, TOK, 256), BF16),
            pltpu.VMEM((2, TOK, 512), F32),
            pltpu.VMEM((2, TOK, 512), BF16),
            pltpu.VMEM((2, 16, 32, 512), BF16),
            dma((5,)), dma((16,)), dma((16,)), dma((2,)), dma((2,)),
            dma((2, 8)), dma((2, 8)), dma((2, 8)), dma((2, 8)), dma((2, 8)), dma((2, 8)),
            dma((2, 16)), dma((2, 16)),
        ],
        compiler_params=pltpu.CompilerParams(
            collective_id=0, has_side_effects=True, vmem_limit_bytes=60 * 1024 * 1024
        ),
        cost_estimate=pl.CostEstimate(flops=10_000_000_000, bytes_accessed=16_000_000, transcendentals=1_000_000),
        name="refresh_and_prefill",
    )(
        hidden_in, lengths, norm_gain.reshape(1, -1), query_weight, key_weight, value_weight, out_weight,
        query_scale.reshape(1, -1), key_scale.reshape(1, -1), value_scale.reshape(1, -1), out_scale.reshape(1, -1),
    )


def solution(mesh):
    in_specs = (
        P("fsdp", None),
        P("fsdp", None),
        P(),
        P(("fsdp", "tp"), None),
        P(("fsdp", "tp"), None),
        P(("fsdp", "tp"), None),
        P(None, ("fsdp", "tp")),
        P(),
        P(),
        P(),
        P(),
    )
    return jax.shard_map(
        shards, mesh=mesh, in_specs=in_specs, out_specs=P(("fsdp", "tp"), None), check_vma=False
    )
```

```python
import math

import jax
import jax.numpy as jnp
from jax import lax
from jax.experimental import pallas as pl
from jax.experimental.pallas import tpu as pltpu
from jax.sharding import PartitionSpec as P

MESH = pl.DeviceIdType.MESH
F32 = jnp.float32
BF16 = jnp.bfloat16

HD = 128
TOK = 512
D = 8192
SATURATE = 448.0
EPSILON = 1e-06
ROPE_BASE = 1000000.0
MASKED_SCORE = -1e30

OUT_TREE = {
    (1, 0): (0, 0, 1),
    (3, 0): (0, 0, -1),
    (0, 1): (0, 0, 0),
    (2, 0): (1, 0, 1),
    (2, 1): (2, 0, 0),
    (1, 1): (0, 1, 1),
    (3, 1): (0, 1, -1),
}
IN_TREE = {**OUT_TREE, (2, 1): (1, 1, 1)}
RING = {(1, 0): (0, 0, 1), (3, 0): (0, 0, -1), (2, 0): (1, 0, 1)}


class Gather:
    def __init__(self, tree, slot, piece, send_sem, recv_sem, plus, minus, pair, source=None):
        self.tree, self.slot, self.piece = tree, slot, piece
        self.send_sem, self.recv_sem = send_sem, recv_sem
        self.to = {1: plus, -1: minus, 0: pair}
        self.source = source

    def index(self, u, dz, h):
        return self.slot(u if h == 0 else (4 - u) % 4, dz)

    def ref(self, u, dz, h):
        return self.piece(self.index(u, dz, h), h)

    def copy(self, u, dz, h):
        su, sdz, step = self.tree[(u, dz)]
        here = there = self.ref(su, sdz, h)
        if self.source is not None and (su, sdz) == (0, 0):
            here = self.source(h, step)
        return pltpu.make_async_remote_copy(
            src_ref=here,
            dst_ref=there,
            send_sem=self.send_sem.at[h, u * 2 + dz],
            recv_sem=self.recv_sem.at[h, u * 2 + dz],
            device_id=self.to[step if h == 0 else -step],
            device_id_type=MESH,
        )

    def send(self, h, *targets):
        for u, dz in targets:
            self.copy(u, dz, h).start()

    def arrived(self, u, dz, h):
        ref = self.ref(u, dz, h)
        pltpu.make_async_remote_copy(
            src_ref=ref,
            dst_ref=ref,
            send_sem=self.send_sem.at[h, u * 2 + dz],
            recv_sem=self.recv_sem.at[h, u * 2 + dz],
            device_id=self.to[1],
            device_id_type=MESH,
        ).wait_recv()

    def sent(self):
        for h in range(2):
            for u, dz in self.tree:
                self.copy(u, dz, h).wait_send()


class Across:
    def __init__(self, gather, piece, send_sem, recv_sem, core_pair):
        self.gather, self.piece = gather, piece
        self.send_sem, self.recv_sem, self.core_pair = send_sem, recv_sem, core_pair
        self.keys = [(0, 0), *gather.tree]

    def copy(self, u, dz, h, other):
        ref = self.piece(self.gather.index(u, dz, h), h, other)
        return pltpu.make_async_remote_copy(
            src_ref=ref, dst_ref=ref, send_sem=self.send_sem.at[h, u * 2 + dz], recv_sem=self.recv_sem.at[h, u * 2 + dz],
            device_id=self.core_pair, device_id_type=MESH,
        )

    def send(self, u, dz, h):
        self.copy(u, dz, h, False).start()

    def arrived(self, u, dz, h):
        self.copy(u, dz, h, True).wait_recv()

    def sent(self):
        for h in range(2):
            for u, dz in self.keys:
                self.copy(u, dz, h, False).wait_send()


def choose(i, values):
    result = values[-1]
    for n in range(len(values) - 2, -1, -1):
        result = jnp.where(i == n, values[n], result)
    return result


def kernel(
    hidden_ref, lengths_ref, gain_ref, wq_ref, wk_ref, wv_ref, wo_ref, qs_ref, ks_ref, vs_ref, os_ref,
    out_ref,
    nrm, raw_q, raw_k, raw_v, raw_o, snd, w_own, w_in, wo, len_t, acc_a, acc_b, cos_t, sin_t, begin_t,
    q_t, kv_t, att_out, att, acc_o, ost, got,
    load_sem, a2a_s, a2a_r, one_s, one_r, core_s, core_r, rows_s, rows_r, ring_s, ring_r, racross_s, racross_r,
    q_s, q_r, o_s, o_r, att_s, att_r, across_s, across_r, fin_s, fin_r,
):
    f = lax.axis_index("fsdp")
    t = lax.axis_index("tp")
    x, zh = f // 2, f % 2
    y, zl, c = t // 4, (t // 2) % 2, t % 2
    rz = (zl + zh) % 2
    role = y * 2 + rz
    hb = role * 2 + c

    def device(ff, tt):
        return {"fsdp": ff, "tp": tt}

    x_plus = device(((x + 1) % 4) * 2 + zh, t)
    x_minus = device(((x + 3) % 4) * 2 + zh, t)
    z_pair = device(x * 2 + 1 - zh, y * 4 + (1 - zl) * 2 + c)
    y_plus = device(f, ((y + 1) % 4) * 4 + zl * 2 + c)
    y_minus = device(f, ((y + 3) % 4) * 4 + zl * 2 + c)
    zl_pair = device(f, y * 4 + (1 - zl) * 2 + c)
    core_pair = device(f, y * 4 + zl * 2 + 1 - c)

    barrier = pltpu.get_barrier_semaphore()
    for other in (x_plus, x_minus, z_pair):
        pl.semaphore_signal(barrier, inc=1, device_id=other, device_id_type=MESH)

    @pl.loop(1, 16)
    def _(i):
        pl.semaphore_signal(barrier, inc=1, device_id=device(f, (t + i) % 16), device_id_type=MESH)

    loads = [
        pltpu.make_async_copy(src, dst, load_sem.at[n])
        for n, (src, dst) in enumerate([(wq_ref, raw_q), (wk_ref, raw_k), (wv_ref, raw_v), (wo_ref, raw_o)])
    ]
    for j in range(8):
        loads.append(pltpu.make_async_copy(hidden_ref.at[:, pl.ds(j * 1024, 1024)], nrm.at[0, j], load_sem.at[4 + j]))
    for load in loads:
        load.start()

    def quantize(weight, inverse):
        return jnp.clip(weight.astype(F32) * inverse, -SATURATE, SATURATE).astype(BF16)

    for load in loads[:3]:
        load.wait()

    @pl.loop(0, 8)
    def _(r):
        for n in range(2):
            for part, place in ((zh, slice(0, 256)), (1 - zh, slice(384, 640))):
                cols = pl.ds(pl.multiple_of((r * 2 + n) * 512 + part * 256, 256), 256)
                snd[r * 2 + n, :, place] = quantize(raw_q[:, cols], 1.0 / qs_ref[:, cols])
        cols = pl.ds(pl.multiple_of(r * 128, 128), 128)
        snd[r * 2, :, 256:384] = quantize(raw_k[:, cols], 1.0 / ks_ref[:, cols])
        snd[r * 2 + 1, :, 256:384] = quantize(raw_v[:, cols], 1.0 / vs_ref[:, cols])

    for n in range(8):
        len_t[0, n:n + 1, :] = jnp.full((1, 128), lengths_ref[0, n], jnp.int32)

    pl.semaphore_wait(barrier, 18)

    def block_copy(i):
        to = (t + i) % 16
        block = ((to // 4) * 2 + ((to // 2) % 2 + zh) % 2) * 2 + to % 2
        return pltpu.make_async_remote_copy(
            src_ref=snd.at[block],
            dst_ref=w_own.at[pl.ds(pl.multiple_of(t * 64, 64), 64)],
            send_sem=a2a_s.at[i],
            recv_sem=a2a_r.at[i],
            device_id=device(f, to),
            device_id_type=MESH,
        )

    @pl.loop(1, 16)
    def _(i):
        block_copy(i).start()

    w_own[pl.ds(pl.multiple_of(t * 64, 64), 64)] = snd[hb]

    def one_copy(n, src, dst, device_id):
        return pltpu.make_async_remote_copy(
            src_ref=src, dst_ref=dst, send_sem=one_s.at[n], recv_sem=one_r.at[n],
            device_id=device_id, device_id_type=MESH,
        )

    len_copy = one_copy(0, len_t.at[0], len_t.at[1], z_pair)
    len_copy.start()

    loads[3].wait()
    chip_cols = pl.ds(pl.multiple_of((f * 8 + t // 2) * 128, 128), 128)
    chip_scale = jnp.broadcast_to(1.0 / os_ref[:, chip_cols], (128, 128))
    on_diagonal = lax.broadcasted_iota(jnp.int32, (128, 128), 0) == lax.broadcasted_iota(jnp.int32, (128, 128), 1)
    chip_column = jnp.sum(jnp.where(on_diagonal, chip_scale, 0.0), axis=1, keepdims=True)
    own_scale = jnp.where(c == 0, chip_column[:64], chip_column[64:])

    @pl.loop(0, 16)
    def _(i):
        cols = pl.ds(pl.multiple_of(i * 512, 512), 512)
        wo[f, :, cols] = quantize(raw_o[:, cols], own_scale)

    def fsdp_slot(dx, dz):
        return ((x + 4 - dx) % 4) * 2 + (zh + dz) % 2

    out_gather = Gather(
        OUT_TREE, fsdp_slot, lambda s, h: wo.at[s, pl.ds(h * 32, 32)], o_s, o_r, x_plus, x_minus, z_pair
    )
    in_gather = Gather(
        IN_TREE, fsdp_slot, lambda s, h: w_in.at[s, pl.ds(h * 512, 512)], q_s, q_r, x_plus, x_minus, z_pair,
        lambda h, step: w_own.at[pl.ds(h * 512, 512), pl.ds(0 if step else 256, 384)],
    )
    row_gather = Gather(
        RING, lambda dy, dz: ((y + 4 - dy) % 4) * 2,
        lambda s, h: nrm.at[1, s + c, pl.ds(h * 256, 256)], ring_s, ring_r, y_plus, y_minus, zl_pair,
    )
    row_across = Across(
        row_gather, lambda s, h, other: nrm.at[1, s + (1 - c if other else c), pl.ds(h * 256, 256)],
        racross_s, racross_r, core_pair,
    )
    att_gather = Gather(
        OUT_TREE, lambda dy, dz: ((y + 4 - dy) % 4) * 2 + (rz + dz) % 2,
        lambda s, h: att.at[s * 2 + c, (zh + h) % 2], att_s, att_r, y_plus, y_minus, zl_pair,
    )
    att_across = Across(
        att_gather, lambda s, h, other: att.at[s * 2 + (1 - c if other else c), (zh + h) % 2],
        across_s, across_r, core_pair,
    )
    for h in range(2):
        out_gather.send(h, (1, 0), (3, 0))

    for load in loads[4:]:
        load.wait()

    def row_copy(h):
        rows = pl.ds(h * 256, 256)
        return pltpu.make_async_remote_copy(
            src_ref=nrm.at[0, y * 2 + c, rows], dst_ref=nrm.at[1, y * 2 + c, rows],
            send_sem=rows_s.at[h], recv_sem=rows_r.at[h], device_id=z_pair, device_id_type=MESH,
        )

    for h in range(2):
        @pl.loop(h * 16, h * 16 + 16)
        def _(i):
            rows = pl.ds(pl.multiple_of(i * 16, 16), 16)
            square = jnp.zeros((16, 1024), F32)
            for j in range(8):
                wide = nrm[0, j, rows, :].astype(F32)
                square += wide * wide
            inverse = lax.rsqrt(jnp.sum(square, axis=1, keepdims=True) * (1.0 / D) + EPSILON)
            for j in range(8):
                wide = nrm[0, j, rows, :].astype(F32)
                nrm[0, j, rows, :] = (wide * inverse * gain_ref[:, j * 1024:(j + 1) * 1024]).astype(BF16)

        row_copy(h).start()

    place = lax.broadcasted_iota(jnp.int32, (TOK, 128), 0)
    lane = lax.broadcasted_iota(jnp.int32, (TOK, 128), 1)

    def tables(replica):
        begin = jnp.zeros((TOK, 128), jnp.int32)
        start = jnp.zeros((1, 128), jnp.int32)
        for n in range(8):
            begin = jnp.where(place >= start, start, begin)
            start = start + len_t[replica, n:n + 1, :]
        begin_t[replica] = begin
        frequency = jnp.exp((lane % 64).astype(F32) * (-2.0 * math.log(ROPE_BASE) / HD))
        angle = (place - begin).astype(F32) * frequency
        cos_t[replica] = jnp.cos(angle)
        sine = jnp.sin(angle)
        sin_t[replica] = jnp.where(lane < 64, -sine, sine)

    tables(0)
    len_copy.wait_recv()
    tables(1)

    for h in range(2):
        @pl.loop(h * 8, h * 8 + 8)
        def _(src):
            @pl.when(src != t)
            def _():
                ref = w_own.at[pl.ds(pl.multiple_of(src * 64, 64), 64)]
                i = (t + 16 - src) % 16
                pltpu.make_async_remote_copy(
                    src_ref=ref, dst_ref=ref, send_sem=a2a_s.at[i], recv_sem=a2a_r.at[i],
                    device_id=core_pair, device_id_type=MESH,
                ).wait_recv()

        in_gather.send(h, (1, 0), (3, 0), (0, 1))

    acc_a[...] = jnp.zeros_like(acc_a)
    acc_b[...] = jnp.zeros_like(acc_b)

    def project(replica, *pieces):
        for dz, total in ((0, acc_a), (1, acc_b)):
            some = [(u, h) for u, z, h in pieces if z == dz and (u, z) != (0, 0)]
            if not some:
                continue
            slots, halves = [in_gather.index(u, dz, h) for u, h in some], [h for _, h in some]

            @pl.loop(0, len(some))
            def _(i):
                s, h = choose(i, slots), choose(i, halves)
                cols = pl.ds(pl.multiple_of(h * 512, 512), 512)
                total[replica] += jnp.dot(nrm[replica, s, :, cols], w_in[s, cols, :], preferred_element_type=F32)

    def project_own(replica):
        @pl.loop(0, 2)
        def _(h):
            cols = pl.ds(pl.multiple_of(h * 512, 512), 512)
            acc_a[replica] += jnp.dot(nrm[replica, f, :, cols], w_own[cols, 0:384], preferred_element_type=F32)

    def halves_of(*places):
        return [(u, dz, h) for u, dz in places for h in range(2)]

    project_own(0)
    for h in range(2):
        row_copy(h).wait_recv()
        row_gather.send(h, (1, 0), (3, 0))
        row_across.send(0, 0, h)
    for h in range(2):
        in_gather.arrived(1, 0, h)
        in_gather.send(h, (2, 0))
    project(0, *halves_of((1, 0)))
    for h in range(2):
        row_gather.arrived(1, 0, h)
        row_gather.send(h, (2, 0))
        row_across.send(1, 0, h)
    for h in range(2):
        in_gather.arrived(0, 1, h)
        in_gather.send(h, (1, 1), (3, 1))
        out_gather.send(h, (0, 1))
    for h in range(2):
        in_gather.arrived(3, 0, h)
    project(0, *halves_of((0, 1), (3, 0)))
    for h in range(2):
        row_gather.arrived(3, 0, h)
        row_across.send(3, 0, h)
    for h in range(2):
        in_gather.arrived(2, 0, h)
    project(0, *halves_of((2, 0)))
    for h in range(2):
        in_gather.arrived(1, 1, h)
        in_gather.send(h, (2, 1))
    project(0, *halves_of((1, 1)))
    for h in range(2):
        row_gather.arrived(2, 0, h)
        row_across.send(2, 0, h)
    for h in range(2):
        for u in range(4):
            row_across.arrived(u, 0, h)
    project_own(1)
    project(1, *halves_of((1, 0), (3, 0), (2, 0), (0, 1), (1, 1)))
    for h in range(2):
        in_gather.arrived(3, 1, h)
    for h in range(2):
        out_gather.arrived(1, 0, h)
        out_gather.send(h, (2, 0))
    for replica in range(2):
        project(replica, *halves_of((3, 1)))
    for h in range(2):
        in_gather.arrived(2, 1, h)
    for h in range(2):
        out_gather.arrived(0, 1, h)
        out_gather.send(h, (1, 1), (3, 1))
    for replica in range(2):
        project(replica, *halves_of((2, 1)))

    def rope(v, replica):
        return v * cos_t[replica] + pltpu.roll(v, 64, axis=1) * sin_t[replica]

    def core_copy(replica, core):
        return pltpu.make_async_remote_copy(
            src_ref=kv_t.at[replica, core], dst_ref=kv_t.at[replica, core],
            send_sem=core_s.at[replica], recv_sem=core_r.at[replica],
            device_id=core_pair, device_id_type=MESH,
        )

    kv_cols = pl.ds(pl.multiple_of(role * 128, 128), 128)
    for replica in (1, 0):
        product = acc_a[replica, :, 256:384] + acc_b[replica, :, 0:128]
        key_raw = (product * ks_ref[:, kv_cols]).astype(BF16).astype(F32)
        value = product * vs_ref[:, kv_cols]
        kv_t[replica, c] = jnp.where(c == 0, rope(key_raw, replica), value).astype(BF16)
        core_copy(replica, c).start()

    for replica in (1, 0):
        for n in range(2):
            product = acc_a[replica, :, n * 128:(n + 1) * 128] + acc_b[replica, :, (n + 1) * 128:(n + 2) * 128]
            scale = qs_ref[:, pl.ds(pl.multiple_of(hb * 512 + zh * 256 + n * 128, 128), 128)]
            q_t[replica, n] = rope(product * scale, replica).astype(BF16)

    def attend(replica, out):
        for n in range(2):
            for b in range(4):
                first = max(0, b * 128 - 256)
                width = (b + 1) * 128 - first
                rows = slice(b * 128, (b + 1) * 128)
                keys = slice(first, first + width)
                scores = lax.dot_general(
                    q_t[replica, n, rows], kv_t[replica, 0, keys], (((1,), (1,)), ((), ())), preferred_element_type=F32
                ) * HD ** (-0.5)
                p = lax.broadcasted_iota(jnp.int32, (128, width), 0) + b * 128
                s = lax.broadcasted_iota(jnp.int32, (128, width), 1) + first
                keep = (s <= p) & (s >= begin_t[replica, rows, 0:1])
                scores = jnp.where(keep, scores, MASKED_SCORE)
                weights = jnp.exp(scores - jnp.max(scores, axis=1, keepdims=True))
                total = jnp.sum(weights, axis=1, keepdims=True)
                mixed = jnp.dot(weights.astype(BF16), kv_t[replica, 1, keys], preferred_element_type=F32)
                out[rows, n * 128:(n + 1) * 128] = (mixed / total).astype(BF16)

    core_copy(1, 1 - c).wait_recv()
    attend(1, att_out)
    att_copy = one_copy(1, att_out, att.at[hb, zh], z_pair)
    att_copy.start()
    core_copy(0, 1 - c).wait_recv()
    attend(0, att.at[hb, zh])
    att_gather.send(0, (1, 0), (3, 0), (0, 1))
    att_across.send(0, 0, 0)
    one_copy(1, att_out, att.at[hb, 1 - zh], z_pair).wait_recv()
    att_gather.send(1, (1, 0), (3, 0), (0, 1))
    att_across.send(0, 0, 1)

    def take(u, dz, h):
        att_gather.arrived(u, dz, h)
        att_across.send(u, dz, h)

    early = [fsdp_slot(dx, dz) for dx, dz in ((0, 0), (1, 0), (3, 0), (0, 1))]
    late = [fsdp_slot(dx, dz) for dx, dz in ((2, 0), (1, 1), (3, 1), (2, 1))]

    def mix(which, slots, pieces):
        roles = [att_gather.index(u, dz, h) for u, dz, h in pieces]
        halves = [(zh + h) % 2 for _, _, h in pieces]
        if which == 0:
            for u, dz, h in pieces:
                att_across.arrived(u, dz, h)

        @pl.loop(0, len(pieces))
        def _(i):
            r, h = choose(i, roles), choose(i, halves)
            for n in range(2):
                cols = pl.ds(pl.multiple_of(r * 1024 + n * 512 + h * 256, 256), 256)
                columns = jnp.concatenate([wo[s, :, cols] for s in slots], axis=0)
                acc_o[which] += lax.dot_general(
                    att[r * 2 + n, h], columns, (((1,), (1,)), ((), ())), preferred_element_type=F32
                )

    def finish(which):
        ost[which] = acc_o[which].astype(BF16)

        @pl.loop(1, 16)
        def _(i):
            final_copy(which, i).start()

        got[which, t] = ost[which, pl.ds(pl.multiple_of(t * 32, 32), 32)]

    def final_copy(which, i):
        to = (t + i) % 16
        return pltpu.make_async_remote_copy(
            src_ref=ost.at[which, pl.ds(pl.multiple_of(to * 32, 32), 32)],
            dst_ref=got.at[which, t],
            send_sem=fin_s.at[which, i],
            recv_sem=fin_r.at[which, i],
            device_id=device(f, to),
            device_id_type=MESH,
        )

    acc_o[...] = jnp.zeros_like(acc_o)
    for h in range(2):
        out_gather.arrived(3, 0, h)
    mix(0, early, [(0, 0, 0), (0, 0, 1)])
    for h in range(2):
        take(1, 0, h)
        att_gather.send(h, (2, 0))
        take(0, 1, h)
        att_gather.send(h, (1, 1), (3, 1))
    mix(0, early, [(1, 0, 0), (1, 0, 1), (0, 1, 0), (0, 1, 1)])
    for h in range(2):
        out_gather.arrived(2, 0, h)
        out_gather.send(h, (2, 1))
    for h in range(2):
        take(3, 0, h)
    for h in range(2):
        take(2, 0, h)
        att_gather.send(h, (2, 1))
    mix(0, early, [(3, 0, 0), (3, 0, 1), (2, 0, 0), (2, 0, 1)])
    for h in range(2):
        for u in (1, 3, 2):
            take(u, 1, h)
    mix(0, early, [(u, 1, h) for u in (1, 3, 2) for h in range(2)])
    finish(0)
    for h in range(2):
        for u in (1, 3, 2):
            out_gather.arrived(u, 1, h)
    mix(1, late, [(u, dz, h) for u in range(4) for dz in range(2) for h in range(2)])
    finish(1)

    def collect(which, offsets):
        @pl.loop(1, 16)
        def _(i):
            ref = got.at[which, (t + 16 - i) % 16]
            pltpu.make_async_remote_copy(
                src_ref=ref, dst_ref=ref, send_sem=fin_s.at[which, i], recv_sem=fin_r.at[which, i],
                device_id=core_pair, device_id_type=MESH,
            ).wait_recv()

        @pl.loop(0, 8)
        def _(k):
            for n, (dx, dz) in enumerate(offsets):
                chip = (k // 2) * 2 + (k % 2 + dz) % 2
                cols = pl.ds(pl.multiple_of((fsdp_slot(dx, dz) * 8 + chip) * 128, 128), 128)
                part = slice(n * 64, (n + 1) * 64)
                both = jnp.concatenate([got[which, k * 2, :, part], got[which, k * 2 + 1, :, part]], axis=1)
                out_ref[:, cols] = (both.astype(F32) * os_ref[:, cols]).astype(BF16)

    collect(0, ((0, 0), (1, 0), (3, 0), (0, 1)))
    collect(1, ((2, 0), (1, 1), (3, 1), (2, 1)))

    @pl.loop(1, 16)
    def _(i):
        block_copy(i).wait_send()
        final_copy(0, i).wait_send()
        final_copy(1, i).wait_send()

    len_copy.wait_send()
    att_copy.wait_send()
    for n in range(2):
        core_copy(n, c).wait_send()
        row_copy(n).wait_send()
    for group in (out_gather, in_gather, row_gather, row_across, att_gather, att_across):
        group.sent()


def shards(
    hidden_in, lengths, norm_gain, query_weight, key_weight, value_weight, out_weight,
    query_scale, key_scale, value_scale, out_scale,
):
    vmem = pl.BlockSpec(memory_space=pltpu.VMEM)
    any_space = pl.BlockSpec(memory_space=pl.ANY)
    smem = pl.BlockSpec(memory_space=pltpu.SMEM)
    dma = pltpu.SemaphoreType.DMA
    return pl.pallas_call(
        kernel,
        out_shape=jax.ShapeDtypeStruct((32, D), BF16),
        in_specs=[any_space, smem, vmem, any_space, any_space, any_space, any_space, vmem, vmem, vmem, vmem],
        out_specs=vmem,
        scratch_shapes=[
            pltpu.VMEM((2, 8, TOK, 1024), BF16),
            pltpu.VMEM((64, D), BF16),
            pltpu.VMEM((64, 1024), BF16),
            pltpu.VMEM((64, 1024), BF16),
            pltpu.VMEM((64, D), BF16),
            pltpu.VMEM((16, 64, 640), BF16),
            pltpu.VMEM((1024, 640), BF16),
            pltpu.VMEM((8, 1024, 384), BF16),
            pltpu.VMEM((8, 64, D), BF16),
            pltpu.VMEM((2, 8, 128), jnp.int32),
            pltpu.VMEM((2, TOK, 384), F32),
            pltpu.VMEM((2, TOK, 384), F32),
            pltpu.VMEM((2, TOK, HD), F32),
            pltpu.VMEM((2, TOK, HD), F32),
            pltpu.VMEM((2, TOK, HD), jnp.int32),
            pltpu.VMEM((2, 2, TOK, HD), BF16),
            pltpu.VMEM((2, 2, TOK, HD), BF16),
            pltpu.VMEM((TOK, 256), BF16),
            pltpu.VMEM((16, 2, TOK, 256), BF16),
            pltpu.VMEM((2, TOK, 256), F32),
            pltpu.VMEM((2, TOK, 256), BF16),
            pltpu.VMEM((2, 16, 32, 256), BF16),
            dma((12,)), dma((16,)), dma((16,)), dma((2,)), dma((2,)), dma((2,)), dma((2,)), dma((2,)), dma((2,)),
            dma((2, 8)), dma((2, 8)), dma((2, 8)), dma((2, 8)),
            dma((2, 8)), dma((2, 8)), dma((2, 8)), dma((2, 8)), dma((2, 8)), dma((2, 8)), dma((2, 8)), dma((2, 8)),
            dma((2, 16)), dma((2, 16)),
        ],
        compiler_params=pltpu.CompilerParams(
            collective_id=0, has_side_effects=True, vmem_limit_bytes=60 * 1024 * 1024
        ),
        cost_estimate=pl.CostEstimate(flops=10_000_000_000, bytes_accessed=16_000_000, transcendentals=1_000_000),
        name="refresh_and_prefill",
    )(
        hidden_in, lengths, norm_gain.reshape(1, -1), query_weight, key_weight, value_weight, out_weight.T,
        query_scale.reshape(1, -1), key_scale.reshape(1, -1), value_scale.reshape(1, -1), out_scale.reshape(1, -1),
    )


def solution(mesh):
    in_specs = (
        P("fsdp", None),
        P("fsdp", None),
        P(),
        P(("fsdp", "tp"), None),
        P(("fsdp", "tp"), None),
        P(("fsdp", "tp"), None),
        P(None, ("fsdp", "tp")),
        P(),
        P(),
        P(),
        P(),
    )
    return jax.shard_map(
        shards, mesh=mesh, in_specs=in_specs, out_specs=P(("fsdp", "tp"), None), check_vma=False
    )
```

```python
import math

import jax
import jax.numpy as jnp
from jax import lax
from jax.experimental import pallas as pl
from jax.experimental.pallas import tpu as pltpu
from jax.sharding import PartitionSpec as P

MESH = pl.DeviceIdType.MESH
F32 = jnp.float32
BF16 = jnp.bfloat16

HD = 128
TOK = 512
D = 8192
SATURATE = 448.0
EPSILON = 1e-06
ROPE_BASE = 1000000.0
MASKED_SCORE = -1e30

OUT_TREE = {
    (1, 0): (0, 0, 1),
    (3, 0): (0, 0, -1),
    (0, 1): (0, 0, 0),
    (2, 0): (1, 0, 1),
    (2, 1): (2, 0, 0),
    (1, 1): (0, 1, 1),
    (3, 1): (0, 1, -1),
}
PAIR_TREE = {**OUT_TREE, (3, 1): (3, 0, 0)}
IN_TREE = {**OUT_TREE, (2, 1): (1, 1, 1)}


class Gather:
    def __init__(self, trees, slot, piece, send_sem, recv_sem, plus, minus, pair, source=None):
        self.trees, self.slot, self.piece = trees, slot, piece
        self.send_sem, self.recv_sem = send_sem, recv_sem
        self.to = {1: plus, -1: minus, 0: pair}
        self.source = source

    def index(self, u, dz, h):
        return self.slot((4 - u) % 4 if h % 2 else u, dz)

    def ref(self, u, dz, h):
        return self.piece(self.index(u, dz, h), h)

    def copy(self, u, dz, h):
        su, sdz, step = self.trees[h][(u, dz)]
        here = there = self.ref(su, sdz, h)
        if self.source is not None and (su, sdz) == (0, 0):
            here = self.source(h, step)
        return pltpu.make_async_remote_copy(
            src_ref=here,
            dst_ref=there,
            send_sem=self.send_sem.at[h, u * 2 + dz],
            recv_sem=self.recv_sem.at[h, u * 2 + dz],
            device_id=self.to[-step if h % 2 else step],
            device_id_type=MESH,
        )

    def send(self, h, *targets):
        for u, dz in targets:
            self.copy(u, dz, h).start()

    def pass_on(self, u, dz, h):
        self.send(h, *[to for to, by in self.trees[h].items() if by[:2] == (u, dz)])

    def arrived(self, u, dz, h):
        ref = self.ref(u, dz, h)
        pltpu.make_async_remote_copy(
            src_ref=ref,
            dst_ref=ref,
            send_sem=self.send_sem.at[h, u * 2 + dz],
            recv_sem=self.recv_sem.at[h, u * 2 + dz],
            device_id=self.to[1],
            device_id_type=MESH,
        ).wait_recv()

    def sent(self):
        for h, tree in enumerate(self.trees):
            for u, dz in tree:
                self.copy(u, dz, h).wait_send()


class Across:
    def __init__(self, gather, piece, send_sem, recv_sem, core_pair):
        self.gather, self.piece = gather, piece
        self.send_sem, self.recv_sem, self.core_pair = send_sem, recv_sem, core_pair
        self.keys = [(0, 0), *OUT_TREE]

    def copy(self, u, dz, h, other):
        ref = self.piece(self.gather.index(u, dz, h), h, other)
        return pltpu.make_async_remote_copy(
            src_ref=ref, dst_ref=ref, send_sem=self.send_sem.at[h, u * 2 + dz], recv_sem=self.recv_sem.at[h, u * 2 + dz],
            device_id=self.core_pair, device_id_type=MESH,
        )

    def send(self, u, dz, h):
        self.copy(u, dz, h, False).start()

    def arrived(self, u, dz, h):
        self.copy(u, dz, h, True).wait_recv()

    def sent(self):
        for h in range(2):
            for u, dz in self.keys:
                self.copy(u, dz, h, False).wait_send()


def choose(i, values):
    result = values[-1]
    for n in range(len(values) - 2, -1, -1):
        result = jnp.where(i == n, values[n], result)
    return result


def kernel(
    hidden_ref, lengths_ref, gain_ref, wq_ref, wk_ref, wv_ref, wo_ref, qs_ref, ks_ref, vs_ref, os_ref,
    out_ref,
    nrm, raw_q, raw_k, raw_v, raw_o, snd, w_own, w_one, w_two, wo, len_t, acc_a, acc_b, acc_c, cos_t, sin_t, begin_t,
    q_t, kv_t, att_out, att, acc_o, ost, got,
    load_sem, a2a_s, a2a_r, one_s, one_r, core_s, core_r, rows_s, rows_r, ring_s, ring_r, racross_s, racross_r,
    one_in_s, one_in_r, two_in_s, two_in_r, o_s, o_r, att_s, att_r, across_s, across_r, fin_s, fin_r,
):
    f = lax.axis_index("fsdp")
    t = lax.axis_index("tp")
    x, zh = f // 2, f % 2
    y, zl, c = t // 4, (t // 2) % 2, t % 2
    rz = (zl + zh) % 2
    role = y * 2 + rz
    hb = role * 2 + c

    def device(ff, tt):
        return {"fsdp": ff, "tp": tt}

    x_plus = device(((x + 1) % 4) * 2 + zh, t)
    x_minus = device(((x + 3) % 4) * 2 + zh, t)
    z_pair = device(x * 2 + 1 - zh, y * 4 + (1 - zl) * 2 + c)
    y_plus = device(f, ((y + 1) % 4) * 4 + zl * 2 + c)
    y_minus = device(f, ((y + 3) % 4) * 4 + zl * 2 + c)
    zl_pair = device(f, y * 4 + (1 - zl) * 2 + c)
    core_pair = device(f, y * 4 + zl * 2 + 1 - c)

    barrier = pltpu.get_barrier_semaphore()
    for other in (x_plus, x_minus, z_pair):
        pl.semaphore_signal(barrier, inc=1, device_id=other, device_id_type=MESH)

    @pl.loop(1, 16)
    def _(i):
        pl.semaphore_signal(barrier, inc=1, device_id=device(f, (t + i) % 16), device_id_type=MESH)

    loads = [
        pltpu.make_async_copy(src, dst, load_sem.at[n])
        for n, (src, dst) in enumerate([(wo_ref, raw_o), (wq_ref, raw_q), (wk_ref, raw_k), (wv_ref, raw_v)])
    ]
    for j in range(8):
        loads.append(pltpu.make_async_copy(hidden_ref.at[:, pl.ds(j * 1024, 1024)], nrm.at[0, j], load_sem.at[4 + j]))
    for load in loads:
        load.start()

    def quantize(weight, inverse):
        return jnp.clip(weight.astype(F32) * inverse, -SATURATE, SATURATE).astype(BF16)

    def fsdp_slot(dx, dz):
        return ((x + 4 - dx) % 4) * 2 + (zh + dz) % 2

    out_gather = Gather(
        [OUT_TREE] * 2 + [PAIR_TREE] * 2, fsdp_slot, lambda s, h: wo.at[s, pl.ds(h * 16, 16)], o_s, o_r,
        x_plus, x_minus, z_pair,
    )
    one_gather = Gather(
        [IN_TREE] * 2, fsdp_slot, lambda s, h: w_one.at[s, pl.ds(h * 512, 512)], one_in_s, one_in_r, x_plus, x_minus, z_pair,
        lambda h, step: w_own.at[pl.ds(h * 512, 512), pl.ds(128 if step else 256, 256)],
    )
    two_gather = Gather(
        [IN_TREE] * 2, fsdp_slot, lambda s, h: w_two.at[s, pl.ds(h * 512, 512)], two_in_s, two_in_r, x_plus, x_minus, z_pair,
        lambda h, step: w_own.at[pl.ds(h * 512, 512), pl.ds(0 if step else 512, 128)],
    )
    def chip_slot(dy, dz):
        return ((y + 4 - dy) % 4) * 2 + (zl + dz) % 2

    def row_piece(s, h, core):
        return nrm.at[1, s, pl.ds(h * 256, 256), pl.ds(pl.multiple_of(core * 512, 512), 512)]

    row_gather = Gather(
        [OUT_TREE] * 2, chip_slot, lambda s, h: row_piece(s, h, c), ring_s, ring_r, y_plus, y_minus, zl_pair
    )
    row_across = Across(
        row_gather, lambda s, h, other: row_piece(s, h, 1 - c if other else c), racross_s, racross_r, core_pair
    )
    def att_slot(dy, dz):
        return ((y + 4 - dy) % 4) * 2 + (rz + dz) % 2

    def att_piece(s, core, half, n):
        return att.at[s, :, pl.ds(pl.multiple_of(core * 512 + half * 256 + n * 128, 128), 128)]

    att_gathers = [
        Gather(
            [OUT_TREE] * 2, att_slot, lambda s, h, n=n: att_piece(s, c, (zh + h) % 2, n),
            att_s.at[n], att_r.at[n], y_plus, y_minus, zl_pair,
        )
        for n in range(2)
    ]
    att_acrosses = [
        Across(
            att_gathers[n], lambda s, h, other, n=n: att_piece(s, 1 - c if other else c, (zh + h) % 2, n),
            across_s.at[n], across_r.at[n], core_pair,
        )
        for n in range(2)
    ]

    loads[0].wait()
    chip_cols = pl.ds(pl.multiple_of((f * 8 + t // 2) * 128, 128), 128)
    chip_scale = jnp.broadcast_to(1.0 / os_ref[:, chip_cols], (128, 128))
    on_diagonal = lax.broadcasted_iota(jnp.int32, (128, 128), 0) == lax.broadcasted_iota(jnp.int32, (128, 128), 1)
    chip_column = jnp.sum(jnp.where(on_diagonal, chip_scale, 0.0), axis=1, keepdims=True)
    own_scale = jnp.where(c == 0, chip_column[:64], chip_column[64:])

    @pl.loop(0, 16)
    def _(i):
        cols = pl.ds(pl.multiple_of(i * 512, 512), 512)
        wo[f, :, cols] = quantize(raw_o[:, cols], own_scale)

    pl.semaphore_wait(barrier, 18)
    for place in ((1, 0), (3, 0)):
        for h in range(4):
            out_gather.send(h, place)
    for h in range(2):
        out_gather.send(h, (0, 1))

    for load in loads[1:4]:
        load.wait()

    @pl.loop(0, 8)
    def _(r):
        for n in range(2):
            for part, head, place in ((zh, 1, 0), (zh, 0, 128), (1 - zh, 0, 384), (1 - zh, 1, 512)):
                cols = pl.ds(pl.multiple_of((r * 2 + n) * 512 + part * 256 + head * 128, 128), 128)
                snd[r * 2 + n, :, place:place + 128] = quantize(raw_q[:, cols], 1.0 / qs_ref[:, cols])
        cols = pl.ds(pl.multiple_of(r * 128, 128), 128)
        snd[r * 2, :, 256:384] = quantize(raw_k[:, cols], 1.0 / ks_ref[:, cols])
        snd[r * 2 + 1, :, 256:384] = quantize(raw_v[:, cols], 1.0 / vs_ref[:, cols])

    for n in range(8):
        len_t[0, n:n + 1, :] = jnp.full((1, 128), lengths_ref[0, n], jnp.int32)

    def block_copy(i):
        to = (t + i) % 16
        block = ((to // 4) * 2 + ((to // 2) % 2 + zh) % 2) * 2 + to % 2
        return pltpu.make_async_remote_copy(
            src_ref=snd.at[block],
            dst_ref=w_own.at[pl.ds(pl.multiple_of(t * 64, 64), 64)],
            send_sem=a2a_s.at[i],
            recv_sem=a2a_r.at[i],
            device_id=device(f, to),
            device_id_type=MESH,
        )

    @pl.loop(1, 16)
    def _(i):
        block_copy(i).start()

    w_own[pl.ds(pl.multiple_of(t * 64, 64), 64)] = snd[hb]

    def one_copy(n, src, dst, device_id):
        return pltpu.make_async_remote_copy(
            src_ref=src, dst_ref=dst, send_sem=one_s.at[n], recv_sem=one_r.at[n],
            device_id=device_id, device_id_type=MESH,
        )

    len_copy = one_copy(0, len_t.at[0], len_t.at[1], z_pair)
    len_copy.start()

    for load in loads[4:]:
        load.wait()

    def row_copy(h, chip):
        rows, cols = pl.ds(h * 256, 256), pl.ds(pl.multiple_of(c * 512, 512), 512)
        return pltpu.make_async_remote_copy(
            src_ref=nrm.at[0, chip, rows, cols], dst_ref=nrm.at[1, chip, rows, cols],
            send_sem=rows_s.at[h], recv_sem=rows_r.at[h], device_id=z_pair, device_id_type=MESH,
        )

    for h in range(2):
        @pl.loop(h * 16, h * 16 + 16)
        def _(i):
            rows = pl.ds(pl.multiple_of(i * 16, 16), 16)
            square = jnp.zeros((16, 1024), F32)
            for j in range(8):
                wide = nrm[0, j, rows, :].astype(F32)
                square += wide * wide
            inverse = lax.rsqrt(jnp.sum(square, axis=1, keepdims=True) * (1.0 / D) + EPSILON)
            for j in range(8):
                wide = nrm[0, j, rows, :].astype(F32)
                nrm[0, j, rows, :] = (wide * inverse * gain_ref[:, j * 1024:(j + 1) * 1024]).astype(BF16)

        row_copy(h, y * 2 + 1 - zl).start()

    place = lax.broadcasted_iota(jnp.int32, (TOK, 128), 0)
    lane = lax.broadcasted_iota(jnp.int32, (TOK, 128), 1)

    def tables(replica):
        begin = jnp.zeros((TOK, 128), jnp.int32)
        start = jnp.zeros((1, 128), jnp.int32)
        for n in range(8):
            begin = jnp.where(place >= start, start, begin)
            start = start + len_t[replica, n:n + 1, :]
        begin_t[replica] = begin
        frequency = jnp.exp((lane % 64).astype(F32) * (-2.0 * math.log(ROPE_BASE) / HD))
        angle = (place - begin).astype(F32) * frequency
        cos_t[replica] = jnp.cos(angle)
        sine = jnp.sin(angle)
        sin_t[replica] = jnp.where(lane < 64, -sine, sine)

    tables(0)
    len_copy.wait_recv()
    tables(1)

    def row_take(h):
        row_copy(h, y * 2 + zl).wait_recv()
        row_gather.send(h, (1, 0), (0, 1))
        row_across.send(0, 0, h)

    def row_wait(u, dz):
        for h in range(2):
            row_gather.arrived(u, dz, h)
            row_gather.pass_on(u, dz, h)
            row_across.send(u, dz, h)

    row_take(0)

    for h in range(2):
        @pl.loop(h * 8, h * 8 + 8)
        def _(src):
            @pl.when(src != t)
            def _():
                ref = w_own.at[pl.ds(pl.multiple_of(src * 64, 64), 64)]
                i = (t + 16 - src) % 16
                pltpu.make_async_remote_copy(
                    src_ref=ref, dst_ref=ref, send_sem=a2a_s.at[i], recv_sem=a2a_r.at[i],
                    device_id=core_pair, device_id_type=MESH,
                ).wait_recv()

    def open_with(gather, *places):
        for place in places:
            for h in range(2):
                gather.send(h, place)

    open_with(one_gather, (1, 0), (0, 1), (3, 0))
    open_with(two_gather, (0, 1))
    for h in range(2, 4):
        out_gather.send(h, (0, 1))
    row_take(1)
    open_with(row_gather, (3, 0))

    for total in (acc_a, acc_b, acc_c):
        total[...] = jnp.zeros_like(total)

    def project(gather, replica, places):
        for dz in range(2):
            some = [(u, h) for u, z in places for h in range(2) if z == dz and (u, z) != (0, 0)]
            if not some:
                continue
            slots, halves = [gather.index(u, dz, h) for u, h in some], [h for _, h in some]
            weight, total = (w_one, (acc_a, acc_b)[dz]) if gather is one_gather else (w_two, acc_c)

            @pl.loop(0, len(some))
            def _(i):
                s, h = choose(i, slots), choose(i, halves)
                cols = pl.ds(pl.multiple_of(h * 512, 512), 512)
                total[replica] += jnp.dot(nrm[replica, s, :, cols], weight[s, cols, :], preferred_element_type=F32)

        if (0, 0) in places:
            lanes, total = (slice(128, 384), acc_a) if gather is one_gather else (slice(0, 128), acc_c)

            @pl.loop(0, 2)
            def _(h):
                cols = pl.ds(pl.multiple_of(h * 512, 512), 512)
                total[replica] += jnp.dot(nrm[replica, f, :, cols], w_own[cols, lanes], preferred_element_type=F32)

    def wait(gather, *places):
        for u, dz in places:
            for h in range(len(gather.trees)):
                gather.arrived(u, dz, h)

    def relay(gather, u, dz):
        for h in range(len(gather.trees)):
            gather.arrived(u, dz, h)
            if dz == 0:
                gather.pass_on(u, dz, h)
        if dz == 1 and u == 0:
            for place in ((1, 1), (3, 1)):
                for h, tree in enumerate(gather.trees):
                    if tree[place][:2] == (0, 1):
                        gather.send(h, place)
        elif dz == 1:
            for h in range(len(gather.trees)):
                gather.pass_on(u, dz, h)

    project(one_gather, 0, [(0, 0)])
    row_wait(1, 0)
    relay(one_gather, 1, 0)
    project(one_gather, 0, [(1, 0)])
    row_wait(0, 1)
    relay(one_gather, 0, 1)
    wait(one_gather, (3, 0))
    project(one_gather, 0, [(0, 1), (3, 0)])
    row_wait(3, 0)
    row_wait(2, 0)
    wait(one_gather, (2, 0))
    project(one_gather, 0, [(2, 0)])
    row_wait(1, 1)
    row_wait(3, 1)
    relay(one_gather, 1, 1)
    project(one_gather, 0, [(1, 1)])
    row_wait(2, 1)
    for h in range(2):
        for u in range(4):
            for dz in range(2):
                row_across.arrived(u, dz, h)
    relay(out_gather, 1, 0)
    project(one_gather, 1, [(0, 0), (1, 0), (3, 0)])
    wait(one_gather, (3, 1))
    open_with(two_gather, (1, 0), (3, 0))
    relay(two_gather, 0, 1)
    project(one_gather, 0, [(3, 1)])
    project(one_gather, 1, [(2, 0), (0, 1), (1, 1), (3, 1)])
    wait(one_gather, (2, 1))
    for replica in (1, 0):
        project(one_gather, replica, [(2, 1)])

    def rope(v, replica):
        return v * cos_t[replica] + pltpu.roll(v, 64, axis=1) * sin_t[replica]

    def core_copy(replica, core):
        return pltpu.make_async_remote_copy(
            src_ref=kv_t.at[replica, core], dst_ref=kv_t.at[replica, core],
            send_sem=core_s.at[replica], recv_sem=core_r.at[replica],
            device_id=core_pair, device_id_type=MESH,
        )

    kv_cols = pl.ds(pl.multiple_of(role * 128, 128), 128)
    for replica in (1, 0):
        product = acc_a[replica, :, 128:256] + acc_b[replica, :, 0:128]
        key_raw = (product * ks_ref[:, kv_cols]).astype(BF16).astype(F32)
        value = product * vs_ref[:, kv_cols]
        kv_t[replica, c] = jnp.where(c == 0, rope(key_raw, replica), value).astype(BF16)
        core_copy(replica, c).start()

    def query(replica, n):
        product = acc_c[replica] if n else acc_a[replica, :, 0:128] + acc_b[replica, :, 128:256]
        scale = qs_ref[:, pl.ds(pl.multiple_of(hb * 512 + zh * 256 + n * 128, 128), 128)]
        q_t[replica, n] = rope(product * scale, replica).astype(BF16)

    def attend(replica, n, out):
        query(replica, n)
        for b in range(4):
            first = max(0, b * 128 - 256)
            width = (b + 1) * 128 - first
            rows = slice(b * 128, (b + 1) * 128)
            keys = slice(first, first + width)
            scores = lax.dot_general(
                q_t[replica, n, rows], kv_t[replica, 0, keys], (((1,), (1,)), ((), ())), preferred_element_type=F32
            ) * HD ** (-0.5)
            p = lax.broadcasted_iota(jnp.int32, (128, width), 0) + b * 128
            s = lax.broadcasted_iota(jnp.int32, (128, width), 1) + first
            keep = (s <= p) & (s >= begin_t[replica, rows, 0:1])
            scores = jnp.where(keep, scores, MASKED_SCORE)
            weights = jnp.exp(scores - jnp.max(scores, axis=1, keepdims=True))
            total = jnp.sum(weights, axis=1, keepdims=True)
            mixed = jnp.dot(weights.astype(BF16), kv_t[replica, 1, keys], preferred_element_type=F32)
            out[rows, :] = (mixed / total).astype(BF16)

    def att_copy(n):
        return one_copy(1 + n, att_out.at[n], att_piece(role, c, zh, n), z_pair)

    def att_arrived(n):
        one_copy(1 + n, att_out.at[n], att_piece(role, c, 1 - zh, n), z_pair).wait_recv()
        att_gathers[n].pass_on(0, 0, 1)
        att_acrosses[n].send(0, 0, 1)

    def att_own(n):
        attend(0, n, att_piece(role, c, zh, n))
        att_gathers[n].pass_on(0, 0, 0)
        att_acrosses[n].send(0, 0, 0)

    def take(n, *places):
        for u, dz in places:
            for h in range(2):
                att_gathers[n].arrived(u, dz, h)
                att_gathers[n].pass_on(u, dz, h)
                att_acrosses[n].send(u, dz, h)

    core_copy(1, 1 - c).wait_recv()
    attend(1, 0, att_out.at[0])
    att_copy(0).start()
    relay(out_gather, 3, 0)
    core_copy(0, 1 - c).wait_recv()
    att_own(0)
    att_arrived(0)
    relay(two_gather, 1, 0)
    for h in range(4):
        out_gather.arrived(2, 0, h)
    for h in range(2):
        out_gather.send(h, (2, 1))
    take(0, (1, 0), (0, 1))
    relay(two_gather, 1, 1)
    for replica in (1, 0):
        project(two_gather, replica, [(0, 0), (1, 0), (0, 1), (1, 1)])
    take(0, (3, 0), (2, 0))
    wait(two_gather, (3, 0), (2, 0), (3, 1))
    relay(out_gather, 0, 1)
    for replica in (1, 0):
        project(two_gather, replica, [(3, 0), (2, 0), (3, 1)])
    take(0, (1, 1), (3, 1), (2, 1))
    wait(two_gather, (2, 1))
    for replica in (1, 0):
        project(two_gather, replica, [(2, 1)])
    attend(1, 1, att_out.at[1])
    att_copy(1).start()
    for h in range(2, 4):
        out_gather.send(h, (2, 1))
    att_own(1)
    att_arrived(1)

    early = [fsdp_slot(dx, dz) for dx, dz in ((0, 0), (1, 0), (3, 0), (0, 1))]
    late = [fsdp_slot(dx, dz) for dx, dz in ((2, 0), (1, 1), (3, 1), (2, 1))]

    def mix_head(n, *places):
        for u, dz in places:
            for h in range(2):
                att_acrosses[n].arrived(u, dz, h)
        roles = [att_slot(u, dz) for u, dz in places]

        @pl.loop(0, len(roles))
        def _(i):
            r = choose(i, roles)
            left = jnp.concatenate([att[r, :, k * 256 + n * 128:k * 256 + n * 128 + 128] for k in range(4)], axis=1)
            cols = [pl.ds(pl.multiple_of(r * 1024 + k * 256 + n * 128, 128), 128) for k in range(4)]
            right = jnp.concatenate(
                [jnp.concatenate([wo[s, :, k] for k in cols], axis=1) for s in early], axis=0
            )
            acc_o[0] += lax.dot_general(left, right, (((1,), (1,)), ((), ())), preferred_element_type=F32)

    def mix_late():
        @pl.loop(0, 8)
        def _(r):
            cols = pl.ds(pl.multiple_of(r * 1024, 1024), 1024)
            right = jnp.concatenate([wo[s, :, cols] for s in late], axis=0)
            acc_o[1] += lax.dot_general(att[r], right, (((1,), (1,)), ((), ())), preferred_element_type=F32)

    def finish(which):
        ost[which] = acc_o[which].astype(BF16)

        @pl.loop(1, 16)
        def _(i):
            final_copy(which, i).start()

        got[which, t] = ost[which, pl.ds(pl.multiple_of(t * 32, 32), 32)]

    def final_copy(which, i):
        to = (t + i) % 16
        return pltpu.make_async_remote_copy(
            src_ref=ost.at[which, pl.ds(pl.multiple_of(to * 32, 32), 32)],
            dst_ref=got.at[which, t],
            send_sem=fin_s.at[which, i],
            recv_sem=fin_r.at[which, i],
            device_id=device(f, to),
            device_id_type=MESH,
        )

    acc_o[...] = jnp.zeros_like(acc_o)
    ring = [(0, 0), (1, 0), (3, 0), (2, 0)]
    beyond = [(0, 1), (1, 1), (3, 1), (2, 1)]
    mix_head(0, *ring)
    take(1, (1, 0), (0, 1))
    mix_head(0, *beyond)
    take(1, (3, 0), (2, 0))
    mix_head(1, *ring)
    take(1, (1, 1), (3, 1), (2, 1))
    mix_head(1, *beyond)
    finish(0)
    wait(out_gather, (1, 1), (3, 1), (2, 1))
    mix_late()
    finish(1)

    def collect(which, offsets):
        @pl.loop(1, 16)
        def _(i):
            ref = got.at[which, (t + 16 - i) % 16]
            pltpu.make_async_remote_copy(
                src_ref=ref, dst_ref=ref, send_sem=fin_s.at[which, i], recv_sem=fin_r.at[which, i],
                device_id=core_pair, device_id_type=MESH,
            ).wait_recv()

        @pl.loop(0, 8)
        def _(k):
            for n, (dx, dz) in enumerate(offsets):
                chip = (k // 2) * 2 + (k % 2 + dz) % 2
                cols = pl.ds(pl.multiple_of((fsdp_slot(dx, dz) * 8 + chip) * 128, 128), 128)
                part = slice(n * 64, (n + 1) * 64)
                both = jnp.concatenate([got[which, k * 2, :, part], got[which, k * 2 + 1, :, part]], axis=1)
                out_ref[:, cols] = (both.astype(F32) * os_ref[:, cols]).astype(BF16)

    collect(0, ((0, 0), (1, 0), (3, 0), (0, 1)))
    collect(1, ((2, 0), (1, 1), (3, 1), (2, 1)))

    @pl.loop(1, 16)
    def _(i):
        block_copy(i).wait_send()
        final_copy(0, i).wait_send()
        final_copy(1, i).wait_send()

    len_copy.wait_send()
    att_copy(0).wait_send()
    att_copy(1).wait_send()
    for n in range(2):
        core_copy(n, c).wait_send()
        row_copy(n, y * 2 + 1 - zl).wait_send()
    for group in (out_gather, one_gather, two_gather, row_gather, row_across, *att_gathers, *att_acrosses):
        group.sent()


def shards(
    hidden_in, lengths, norm_gain, query_weight, key_weight, value_weight, out_weight,
    query_scale, key_scale, value_scale, out_scale,
):
    vmem = pl.BlockSpec(memory_space=pltpu.VMEM)
    any_space = pl.BlockSpec(memory_space=pl.ANY)
    smem = pl.BlockSpec(memory_space=pltpu.SMEM)
    dma = pltpu.SemaphoreType.DMA
    return pl.pallas_call(
        kernel,
        out_shape=jax.ShapeDtypeStruct((32, D), BF16),
        in_specs=[any_space, smem, vmem, any_space, any_space, any_space, any_space, vmem, vmem, vmem, vmem],
        out_specs=vmem,
        scratch_shapes=[
            pltpu.VMEM((2, 8, TOK, 1024), BF16),
            pltpu.VMEM((64, D), BF16),
            pltpu.VMEM((64, 1024), BF16),
            pltpu.VMEM((64, 1024), BF16),
            pltpu.VMEM((64, D), BF16),
            pltpu.VMEM((16, 64, 640), BF16),
            pltpu.VMEM((1024, 640), BF16),
            pltpu.VMEM((8, 1024, 256), BF16),
            pltpu.VMEM((8, 1024, 128), BF16),
            pltpu.VMEM((8, 64, D), BF16),
            pltpu.VMEM((2, 8, 128), jnp.int32),
            pltpu.VMEM((2, TOK, 256), F32),
            pltpu.VMEM((2, TOK, 256), F32),
            pltpu.VMEM((2, TOK, HD), F32),
            pltpu.VMEM((2, TOK, HD), F32),
            pltpu.VMEM((2, TOK, HD), F32),
            pltpu.VMEM((2, TOK, HD), jnp.int32),
            pltpu.VMEM((2, 2, TOK, HD), BF16),
            pltpu.VMEM((2, 2, TOK, HD), BF16),
            pltpu.VMEM((2, TOK, HD), BF16),
            pltpu.VMEM((8, TOK, 1024), BF16),
            pltpu.VMEM((2, TOK, 256), F32),
            pltpu.VMEM((2, TOK, 256), BF16),
            pltpu.VMEM((2, 16, 32, 256), BF16),
            dma((12,)), dma((16,)), dma((16,)), dma((3,)), dma((3,)), dma((2,)), dma((2,)), dma((2,)), dma((2,)),
            dma((2, 8)), dma((2, 8)), dma((2, 8)), dma((2, 8)),
            dma((2, 8)), dma((2, 8)), dma((2, 8)), dma((2, 8)), dma((4, 8)), dma((4, 8)),
            dma((2, 2, 8)), dma((2, 2, 8)), dma((2, 2, 8)), dma((2, 2, 8)),
            dma((2, 16)), dma((2, 16)),
        ],
        compiler_params=pltpu.CompilerParams(
            collective_id=0, has_side_effects=True, vmem_limit_bytes=60 * 1024 * 1024
        ),
        cost_estimate=pl.CostEstimate(flops=10_000_000_000, bytes_accessed=16_000_000, transcendentals=1_000_000),
        name="refresh_and_prefill",
    )(
        hidden_in, lengths, norm_gain.reshape(1, -1), query_weight, key_weight, value_weight, out_weight.T,
        query_scale.reshape(1, -1), key_scale.reshape(1, -1), value_scale.reshape(1, -1), out_scale.reshape(1, -1),
    )


def solution(mesh):
    in_specs = (
        P("fsdp", None),
        P("fsdp", None),
        P(),
        P(("fsdp", "tp"), None),
        P(("fsdp", "tp"), None),
        P(("fsdp", "tp"), None),
        P(None, ("fsdp", "tp")),
        P(),
        P(),
        P(),
        P(),
    )
    return jax.shard_map(
        shards, mesh=mesh, in_specs=in_specs, out_specs=P(("fsdp", "tp"), None), check_vma=False
    )
```

```python
import math

import jax
import jax.numpy as jnp
from jax import lax
from jax.experimental import pallas as pl
from jax.experimental.pallas import tpu as pltpu
from jax.sharding import PartitionSpec as P

MESH = pl.DeviceIdType.MESH
F32 = jnp.float32
BF16 = jnp.bfloat16

HD = 128
TOK = 512
D = 8192
SATURATE = 448.0
EPSILON = 1e-06
ROPE_BASE = 1000000.0
MASKED_SCORE = -1e30

OUT_TREE = {
    (1, 0): (0, 0, 1),
    (3, 0): (0, 0, -1),
    (0, 1): (0, 0, 0),
    (2, 0): (1, 0, 1),
    (2, 1): (2, 0, 0),
    (1, 1): (0, 1, 1),
    (3, 1): (0, 1, -1),
}
PAIR_TREE = {**OUT_TREE, (3, 1): (3, 0, 0)}
IN_TREE = {**OUT_TREE, (2, 1): (1, 1, 1)}


class Gather:
    def __init__(self, trees, slot, piece, send_sem, recv_sem, plus, minus, pair, source=None):
        self.trees, self.slot, self.piece = trees, slot, piece
        self.send_sem, self.recv_sem = send_sem, recv_sem
        self.to = {1: plus, -1: minus, 0: pair}
        self.source = source

    def index(self, u, dz, h):
        return self.slot((4 - u) % 4 if h % 2 else u, dz)

    def ref(self, u, dz, h):
        return self.piece(self.index(u, dz, h), h)

    def copy(self, u, dz, h):
        su, sdz, step = self.trees[h][(u, dz)]
        here = there = self.ref(su, sdz, h)
        if self.source is not None and (su, sdz) == (0, 0):
            here = self.source(h, step)
        return pltpu.make_async_remote_copy(
            src_ref=here,
            dst_ref=there,
            send_sem=self.send_sem.at[h, u * 2 + dz],
            recv_sem=self.recv_sem.at[h, u * 2 + dz],
            device_id=self.to[-step if h % 2 else step],
            device_id_type=MESH,
        )

    def send(self, h, *targets):
        for u, dz in targets:
            self.copy(u, dz, h).start()

    def pass_on(self, u, dz, h):
        self.send(h, *[to for to, by in self.trees[h].items() if by[:2] == (u, dz)])

    def arrived(self, u, dz, h):
        ref = self.ref(u, dz, h)
        pltpu.make_async_remote_copy(
            src_ref=ref,
            dst_ref=ref,
            send_sem=self.send_sem.at[h, u * 2 + dz],
            recv_sem=self.recv_sem.at[h, u * 2 + dz],
            device_id=self.to[1],
            device_id_type=MESH,
        ).wait_recv()

    def sent(self):
        for h, tree in enumerate(self.trees):
            for u, dz in tree:
                self.copy(u, dz, h).wait_send()


class Across:
    def __init__(self, gather, piece, send_sem, recv_sem, core_pair):
        self.gather, self.piece = gather, piece
        self.send_sem, self.recv_sem, self.core_pair = send_sem, recv_sem, core_pair
        self.keys = [(0, 0), *OUT_TREE]

    def copy(self, u, dz, h, other):
        ref = self.piece(self.gather.index(u, dz, h), h, other)
        return pltpu.make_async_remote_copy(
            src_ref=ref, dst_ref=ref, send_sem=self.send_sem.at[h, u * 2 + dz], recv_sem=self.recv_sem.at[h, u * 2 + dz],
            device_id=self.core_pair, device_id_type=MESH,
        )

    def send(self, u, dz, h):
        self.copy(u, dz, h, False).start()

    def arrived(self, u, dz, h):
        self.copy(u, dz, h, True).wait_recv()

    def sent(self):
        for h in range(2):
            for u, dz in self.keys:
                self.copy(u, dz, h, False).wait_send()


def choose(i, values):
    result = values[-1]
    for n in range(len(values) - 2, -1, -1):
        result = jnp.where(i == n, values[n], result)
    return result


def kernel(
    hidden_ref, lengths_ref, gain_ref, wq_ref, wk_ref, wv_ref, wo_ref, qs_ref, ks_ref, vs_ref, os_ref,
    out_ref,
    nrm, raw_q, raw_k, raw_v, raw_o, snd, w_own, w_one, w_two, wo, len_t, acc_a, acc_b, acc_c, cos_t, sin_t, begin_t,
    q_t, kv_t, att_out, att, acc_o, ost, got,
    load_sem, a2a_s, a2a_r, one_s, one_r, core_s, core_r, rows_s, rows_r, ring_s, ring_r, racross_s, racross_r,
    one_in_s, one_in_r, two_in_s, two_in_r, o_s, o_r, att_s, att_r, across_s, across_r, fin_s, fin_r,
):
    f = lax.axis_index("fsdp")
    t = lax.axis_index("tp")
    x, zh = f // 2, f % 2
    y, zl, c = t // 4, (t // 2) % 2, t % 2
    rz = (zl + zh) % 2
    role = y * 2 + rz
    hb = role * 2 + c

    def device(ff, tt):
        return {"fsdp": ff, "tp": tt}

    x_plus = device(((x + 1) % 4) * 2 + zh, t)
    x_minus = device(((x + 3) % 4) * 2 + zh, t)
    z_pair = device(x * 2 + 1 - zh, y * 4 + (1 - zl) * 2 + c)
    y_plus = device(f, ((y + 1) % 4) * 4 + zl * 2 + c)
    y_minus = device(f, ((y + 3) % 4) * 4 + zl * 2 + c)
    zl_pair = device(f, y * 4 + (1 - zl) * 2 + c)
    core_pair = device(f, y * 4 + zl * 2 + 1 - c)

    barrier = pltpu.get_barrier_semaphore()
    for other in (x_plus, x_minus, z_pair):
        pl.semaphore_signal(barrier, inc=1, device_id=other, device_id_type=MESH)

    @pl.loop(1, 16)
    def _(i):
        pl.semaphore_signal(barrier, inc=1, device_id=device(f, (t + i) % 16), device_id_type=MESH)

    loads = [
        pltpu.make_async_copy(src, dst, load_sem.at[n])
        for n, (src, dst) in enumerate([(wo_ref, raw_o), (wq_ref, raw_q), (wk_ref, raw_k), (wv_ref, raw_v)])
    ]
    for j in range(8):
        loads.append(pltpu.make_async_copy(hidden_ref.at[:, pl.ds(j * 1024, 1024)], nrm.at[0, j], load_sem.at[4 + j]))
    for load in loads:
        load.start()

    def quantize(weight, inverse):
        return jnp.clip(weight.astype(F32) * inverse, -SATURATE, SATURATE).astype(BF16)

    def fsdp_slot(dx, dz):
        return ((x + 4 - dx) % 4) * 2 + (zh + dz) % 2

    out_gather = Gather(
        [OUT_TREE] * 2 + [PAIR_TREE] * 2, fsdp_slot, lambda s, h: wo.at[s, pl.ds(h * 16, 16)], o_s, o_r,
        x_plus, x_minus, z_pair,
    )
    one_gather = Gather(
        [IN_TREE] * 2, fsdp_slot, lambda s, h: w_one.at[s, pl.ds(h * 512, 512)], one_in_s, one_in_r, x_plus, x_minus, z_pair,
        lambda h, step: w_own.at[pl.ds(h * 512, 512), pl.ds(128 if step else 256, 256)],
    )
    two_gather = Gather(
        [IN_TREE] * 2, fsdp_slot, lambda s, h: w_two.at[s, pl.ds(h * 512, 512)], two_in_s, two_in_r, x_plus, x_minus, z_pair,
        lambda h, step: w_own.at[pl.ds(h * 512, 512), pl.ds(0 if step else 512, 128)],
    )
    def chip_slot(dy, dz):
        return ((y + 4 - dy) % 4) * 2 + (zl + dz) % 2

    def row_piece(s, h, core):
        return nrm.at[1, s, pl.ds(h * 256, 256), pl.ds(pl.multiple_of(core * 512, 512), 512)]

    row_gather = Gather(
        [OUT_TREE] * 2, chip_slot, lambda s, h: row_piece(s, h, c), ring_s, ring_r, y_plus, y_minus, zl_pair
    )
    row_across = Across(
        row_gather, lambda s, h, other: row_piece(s, h, 1 - c if other else c), racross_s, racross_r, core_pair
    )
    def att_slot(dy, dz):
        return ((y + 4 - dy) % 4) * 2 + (rz + dz) % 2

    def att_piece(s, core, half, n):
        return att.at[s, :, pl.ds(pl.multiple_of(core * 512 + half * 256 + n * 128, 128), 128)]

    att_gathers = [
        Gather(
            [OUT_TREE] * 2, att_slot, lambda s, h, n=n: att_piece(s, c, (zh + h) % 2, n),
            att_s.at[n], att_r.at[n], y_plus, y_minus, zl_pair,
        )
        for n in range(2)
    ]
    att_acrosses = [
        Across(
            att_gathers[n], lambda s, h, other, n=n: att_piece(s, 1 - c if other else c, (zh + h) % 2, n),
            across_s.at[n], across_r.at[n], core_pair,
        )
        for n in range(2)
    ]

    loads[0].wait()
    chip_cols = pl.ds(pl.multiple_of((f * 8 + t // 2) * 128, 128), 128)
    chip_scale = jnp.broadcast_to(1.0 / os_ref[:, chip_cols], (128, 128))
    on_diagonal = lax.broadcasted_iota(jnp.int32, (128, 128), 0) == lax.broadcasted_iota(jnp.int32, (128, 128), 1)
    chip_column = jnp.sum(jnp.where(on_diagonal, chip_scale, 0.0), axis=1, keepdims=True)
    own_scale = jnp.where(c == 0, chip_column[:64], chip_column[64:])

    @pl.loop(0, 16)
    def _(i):
        cols = pl.ds(pl.multiple_of(i * 512, 512), 512)
        wo[f, :, cols] = quantize(raw_o[:, cols], own_scale)

    pl.semaphore_wait(barrier, 18)
    for place in ((1, 0), (3, 0)):
        for h in range(4):
            out_gather.send(h, place)
    out_gather.send(0, (0, 1))

    for load in loads[1:4]:
        load.wait()

    @pl.loop(0, 8)
    def _(r):
        for n in range(2):
            for part, head, place in ((zh, 1, 0), (zh, 0, 128), (1 - zh, 0, 384), (1 - zh, 1, 512)):
                cols = pl.ds(pl.multiple_of((r * 2 + n) * 512 + part * 256 + head * 128, 128), 128)
                snd[r * 2 + n, :, place:place + 128] = quantize(raw_q[:, cols], 1.0 / qs_ref[:, cols])
        cols = pl.ds(pl.multiple_of(r * 128, 128), 128)
        snd[r * 2, :, 256:384] = quantize(raw_k[:, cols], 1.0 / ks_ref[:, cols])
        snd[r * 2 + 1, :, 256:384] = quantize(raw_v[:, cols], 1.0 / vs_ref[:, cols])

    for n in range(8):
        len_t[0, n:n + 1, :] = jnp.full((1, 128), lengths_ref[0, n], jnp.int32)

    def block_copy(i):
        to = (t + i) % 16
        block = ((to // 4) * 2 + ((to // 2) % 2 + zh) % 2) * 2 + to % 2
        return pltpu.make_async_remote_copy(
            src_ref=snd.at[block],
            dst_ref=w_own.at[pl.ds(pl.multiple_of(t * 64, 64), 64)],
            send_sem=a2a_s.at[i],
            recv_sem=a2a_r.at[i],
            device_id=device(f, to),
            device_id_type=MESH,
        )

    @pl.loop(1, 16)
    def _(i):
        block_copy(i).start()

    w_own[pl.ds(pl.multiple_of(t * 64, 64), 64)] = snd[hb]

    def one_copy(n, src, dst, device_id):
        return pltpu.make_async_remote_copy(
            src_ref=src, dst_ref=dst, send_sem=one_s.at[n], recv_sem=one_r.at[n],
            device_id=device_id, device_id_type=MESH,
        )

    len_copy = one_copy(0, len_t.at[0], len_t.at[1], z_pair)
    len_copy.start()

    for load in loads[4:]:
        load.wait()

    def row_copy(h, chip):
        rows, cols = pl.ds(h * 256, 256), pl.ds(pl.multiple_of(c * 512, 512), 512)
        return pltpu.make_async_remote_copy(
            src_ref=nrm.at[0, chip, rows, cols], dst_ref=nrm.at[1, chip, rows, cols],
            send_sem=rows_s.at[h], recv_sem=rows_r.at[h], device_id=z_pair, device_id_type=MESH,
        )

    for h in range(2):
        @pl.loop(h * 16, h * 16 + 16)
        def _(i):
            rows = pl.ds(pl.multiple_of(i * 16, 16), 16)
            square = jnp.zeros((16, 1024), F32)
            for j in range(8):
                wide = nrm[0, j, rows, :].astype(F32)
                square += wide * wide
            inverse = lax.rsqrt(jnp.sum(square, axis=1, keepdims=True) * (1.0 / D) + EPSILON)
            for j in range(8):
                wide = nrm[0, j, rows, :].astype(F32)
                nrm[0, j, rows, :] = (wide * inverse * gain_ref[:, j * 1024:(j + 1) * 1024]).astype(BF16)

        row_copy(h, y * 2 + 1 - zl).start()

    place = lax.broadcasted_iota(jnp.int32, (TOK, 128), 0)
    lane = lax.broadcasted_iota(jnp.int32, (TOK, 128), 1)

    def tables(replica):
        begin = jnp.zeros((TOK, 128), jnp.int32)
        start = jnp.zeros((1, 128), jnp.int32)
        for n in range(8):
            begin = jnp.where(place >= start, start, begin)
            start = start + len_t[replica, n:n + 1, :]
        begin_t[replica] = begin
        frequency = jnp.exp((lane % 64).astype(F32) * (-2.0 * math.log(ROPE_BASE) / HD))
        angle = (place - begin).astype(F32) * frequency
        cos_t[replica] = jnp.cos(angle)
        sine = jnp.sin(angle)
        sin_t[replica] = jnp.where(lane < 64, -sine, sine)

    tables(0)
    len_copy.wait_recv()
    tables(1)

    def row_take(h):
        row_copy(h, y * 2 + zl).wait_recv()
        row_gather.send(h, (1, 0), (0, 1))
        row_across.send(0, 0, h)

    def row_wait(u, dz):
        for h in range(2):
            row_gather.arrived(u, dz, h)
            row_gather.pass_on(u, dz, h)
            row_across.send(u, dz, h)

    row_take(0)

    for h in range(2):
        @pl.loop(h * 8, h * 8 + 8)
        def _(src):
            @pl.when(src != t)
            def _():
                ref = w_own.at[pl.ds(pl.multiple_of(src * 64, 64), 64)]
                i = (t + 16 - src) % 16
                pltpu.make_async_remote_copy(
                    src_ref=ref, dst_ref=ref, send_sem=a2a_s.at[i], recv_sem=a2a_r.at[i],
                    device_id=core_pair, device_id_type=MESH,
                ).wait_recv()

    def open_with(gather, *places):
        for place in places:
            for h in range(2):
                gather.send(h, place)

    open_with(one_gather, (1, 0), (0, 1), (3, 0))
    open_with(two_gather, (0, 1))
    for h in range(1, 4):
        out_gather.send(h, (0, 1))
    row_take(1)
    open_with(row_gather, (3, 0))

    for total in (acc_a, acc_b, acc_c):
        total[...] = jnp.zeros_like(total)

    def project(gather, replica, places):
        for dz in range(2):
            some = [(u, h) for u, z in places for h in range(2) if z == dz and (u, z) != (0, 0)]
            if not some:
                continue
            slots, halves = [gather.index(u, dz, h) for u, h in some], [h for _, h in some]
            weight, total = (w_one, (acc_a, acc_b)[dz]) if gather is one_gather else (w_two, acc_c)

            @pl.loop(0, len(some))
            def _(i):
                s, h = choose(i, slots), choose(i, halves)
                cols = pl.ds(pl.multiple_of(h * 512, 512), 512)
                total[replica] += jnp.dot(nrm[replica, s, :, cols], weight[s, cols, :], preferred_element_type=F32)

        if (0, 0) in places:
            lanes, total = (slice(128, 384), acc_a) if gather is one_gather else (slice(0, 128), acc_c)

            @pl.loop(0, 2)
            def _(h):
                cols = pl.ds(pl.multiple_of(h * 512, 512), 512)
                total[replica] += jnp.dot(nrm[replica, f, :, cols], w_own[cols, lanes], preferred_element_type=F32)

    def project_items(gather, replicas, places):
        first = gather is one_gather
        for dz in range(2):
            slots = [fsdp_slot(u, z) for u, z in places if z == dz and (u, z) != (0, 0)]
            if not slots:
                continue
            weight, total = (w_one, (acc_a, acc_b)[dz]) if first else (w_two, acc_c)

            @pl.loop(0, len(slots) * len(replicas))
            def _(i):
                s = choose(i % len(slots), slots)
                replica = choose(i // len(slots), replicas)
                total[replica] += jnp.dot(nrm[replica, s], weight[s], preferred_element_type=F32)

        if (0, 0) in places:
            lanes, total = (slice(128, 384), acc_a) if first else (slice(0, 128), acc_c)

            @pl.loop(0, len(replicas))
            def _(i):
                replica = choose(i, replicas)
                total[replica] += jnp.dot(nrm[replica, f], w_own[:, lanes], preferred_element_type=F32)

    def wait(gather, *places):
        for u, dz in places:
            for h in range(len(gather.trees)):
                gather.arrived(u, dz, h)

    def relay(gather, u, dz):
        for h in range(len(gather.trees)):
            gather.arrived(u, dz, h)
            if dz == 0:
                gather.pass_on(u, dz, h)
        if dz == 1 and u == 0:
            for place in ((1, 1), (3, 1)):
                for h, tree in enumerate(gather.trees):
                    if tree[place][:2] == (0, 1):
                        gather.send(h, place)
        elif dz == 1:
            for h in range(len(gather.trees)):
                gather.pass_on(u, dz, h)

    def out_relay(u, dz, *parts):
        for h in parts:
            out_gather.arrived(u, dz, h)
            out_gather.pass_on(u, dz, h)

    project(one_gather, 0, [(0, 0)])
    row_wait(1, 0)
    relay(one_gather, 1, 0)
    project(one_gather, 0, [(1, 0)])
    row_wait(0, 1)
    relay(one_gather, 0, 1)
    wait(one_gather, (3, 0))
    project(one_gather, 0, [(0, 1), (3, 0)])
    row_wait(3, 0)
    row_wait(2, 0)
    wait(one_gather, (2, 0))
    project(one_gather, 0, [(2, 0)])
    relay(one_gather, 1, 1)
    out_relay(1, 0, 0, 1)
    for h in range(4):
        out_gather.arrived(3, 0, h)
    out_gather.pass_on(3, 0, 2)
    project(one_gather, 0, [(1, 1)])
    row_wait(1, 1)
    wait(one_gather, (3, 1))
    open_with(two_gather, (1, 0), (3, 0))
    relay(two_gather, 0, 1)
    project(one_gather, 0, [(3, 1)])
    row_wait(3, 1)
    row_wait(2, 1)
    for h in range(2):
        for u in range(4):
            for dz in range(2):
                row_across.arrived(u, dz, h)
    project_items(one_gather, (1,), [(0, 0), (1, 0), (3, 0), (2, 0), (0, 1), (1, 1), (3, 1)])
    wait(one_gather, (2, 1))
    project_items(one_gather, (1, 0), [(2, 1)])

    def rope(v, replica):
        return v * cos_t[replica] + pltpu.roll(v, 64, axis=1) * sin_t[replica]

    def core_copy(replica, core):
        return pltpu.make_async_remote_copy(
            src_ref=kv_t.at[replica, core], dst_ref=kv_t.at[replica, core],
            send_sem=core_s.at[replica], recv_sem=core_r.at[replica],
            device_id=core_pair, device_id_type=MESH,
        )

    kv_cols = pl.ds(pl.multiple_of(role * 128, 128), 128)
    for replica in (1, 0):
        product = acc_a[replica, :, 128:256] + acc_b[replica, :, 0:128]
        key_raw = (product * ks_ref[:, kv_cols]).astype(BF16).astype(F32)
        value = product * vs_ref[:, kv_cols]
        kv_t[replica, c] = jnp.where(c == 0, rope(key_raw, replica), value).astype(BF16)
        core_copy(replica, c).start()

    def query(replica, n):
        product = acc_c[replica] if n else acc_a[replica, :, 0:128] + acc_b[replica, :, 128:256]
        scale = qs_ref[:, pl.ds(pl.multiple_of(hb * 512 + zh * 256 + n * 128, 128), 128)]
        q_t[replica, n] = rope(product * scale, replica).astype(BF16)

    def attend(replica, n, out):
        query(replica, n)
        for b in range(4):
            first = max(0, b * 128 - 256)
            width = (b + 1) * 128 - first
            rows = slice(b * 128, (b + 1) * 128)
            keys = slice(first, first + width)
            scores = lax.dot_general(
                q_t[replica, n, rows], kv_t[replica, 0, keys], (((1,), (1,)), ((), ())), preferred_element_type=F32
            ) * HD ** (-0.5)
            p = lax.broadcasted_iota(jnp.int32, (128, width), 0) + b * 128
            s = lax.broadcasted_iota(jnp.int32, (128, width), 1) + first
            keep = (s <= p) & (s >= begin_t[replica, rows, 0:1])
            scores = jnp.where(keep, scores, MASKED_SCORE)
            weights = jnp.exp(scores - jnp.max(scores, axis=1, keepdims=True))
            total = jnp.sum(weights, axis=1, keepdims=True)
            mixed = jnp.dot(weights.astype(BF16), kv_t[replica, 1, keys], preferred_element_type=F32)
            out[rows, :] = (mixed / total).astype(BF16)

    def att_copy(n):
        return one_copy(1 + n, att_out.at[n], att_piece(role, c, zh, n), z_pair)

    def att_arrived(n):
        one_copy(1 + n, att_out.at[n], att_piece(role, c, 1 - zh, n), z_pair).wait_recv()
        att_gathers[n].pass_on(0, 0, 1)
        att_acrosses[n].send(0, 0, 1)

    def att_own(n):
        attend(0, n, att_piece(role, c, zh, n))
        att_gathers[n].pass_on(0, 0, 0)
        att_acrosses[n].send(0, 0, 0)

    def take(n, *places):
        for u, dz in places:
            for h in range(2):
                att_gathers[n].arrived(u, dz, h)
                att_gathers[n].pass_on(u, dz, h)
                att_acrosses[n].send(u, dz, h)

    core_copy(1, 1 - c).wait_recv()
    attend(1, 0, att_out.at[0])
    att_copy(0).start()
    out_gather.pass_on(3, 0, 3)
    core_copy(0, 1 - c).wait_recv()
    att_own(0)
    att_arrived(0)
    relay(two_gather, 1, 0)
    out_relay(2, 0, 0, 1)
    take(0, (1, 0), (0, 1))
    relay(two_gather, 1, 1)
    out_relay(1, 0, 2, 3)
    relay(out_gather, 0, 1)
    project_items(two_gather, (1, 0), [(0, 0), (0, 1)])
    take(0, (3, 0), (2, 0))
    wait(two_gather, (3, 0), (2, 0), (3, 1))
    project_items(two_gather, (1, 0), [(1, 0), (3, 0), (2, 0), (1, 1), (3, 1)])
    take(0, (1, 1), (3, 1), (2, 1))
    wait(two_gather, (2, 1))
    project_items(two_gather, (1, 0), [(2, 1)])
    attend(1, 1, att_out.at[1])
    att_copy(1).start()
    att_own(1)
    att_arrived(1)

    early = [fsdp_slot(dx, dz) for dx, dz in ((0, 0), (1, 0), (3, 0), (0, 1))]
    late = [fsdp_slot(dx, dz) for dx, dz in ((2, 0), (1, 1), (3, 1), (2, 1))]

    def mix_head(n, *places):
        for u, dz in places:
            for h in range(2):
                att_acrosses[n].arrived(u, dz, h)
        roles = [att_slot(u, dz) for u, dz in places]

        @pl.loop(0, len(roles))
        def _(i):
            r = choose(i, roles)
            left = jnp.concatenate([att[r, :, k * 256 + n * 128:k * 256 + n * 128 + 128] for k in range(4)], axis=1)
            cols = [pl.ds(pl.multiple_of(r * 1024 + k * 256 + n * 128, 128), 128) for k in range(4)]
            right = jnp.concatenate(
                [jnp.concatenate([wo[s, :, k] for k in cols], axis=1) for s in early], axis=0
            )
            acc_o[0] += lax.dot_general(left, right, (((1,), (1,)), ((), ())), preferred_element_type=F32)

    def mix_late():
        @pl.loop(0, 8)
        def _(r):
            cols = pl.ds(pl.multiple_of(r * 1024, 1024), 1024)
            right = jnp.concatenate([wo[s, :, cols] for s in late], axis=0)
            acc_o[1] += lax.dot_general(att[r], right, (((1,), (1,)), ((), ())), preferred_element_type=F32)

    def finish(which):
        ost[which] = acc_o[which].astype(BF16)

        @pl.loop(1, 16)
        def _(i):
            final_copy(which, i).start()

        got[which, t] = ost[which, pl.ds(pl.multiple_of(t * 32, 32), 32)]

    def final_copy(which, i):
        to = (t + i) % 16
        return pltpu.make_async_remote_copy(
            src_ref=ost.at[which, pl.ds(pl.multiple_of(to * 32, 32), 32)],
            dst_ref=got.at[which, t],
            send_sem=fin_s.at[which, i],
            recv_sem=fin_r.at[which, i],
            device_id=device(f, to),
            device_id_type=MESH,
        )

    acc_o[...] = jnp.zeros_like(acc_o)
    ring = [(0, 0), (1, 0), (3, 0), (2, 0)]
    beyond = [(0, 1), (1, 1), (3, 1), (2, 1)]
    mix_head(0, *ring)
    take(1, (1, 0), (0, 1))
    out_relay(2, 0, 2, 3)
    mix_head(0, *beyond)
    take(1, (3, 0), (2, 0))
    mix_head(1, *ring)
    take(1, (1, 1), (3, 1), (2, 1))
    mix_head(1, *beyond)
    finish(0)
    wait(out_gather, (1, 1), (3, 1), (2, 1))
    mix_late()
    finish(1)

    def collect(which, offsets):
        @pl.loop(1, 16)
        def _(i):
            ref = got.at[which, (t + 16 - i) % 16]
            pltpu.make_async_remote_copy(
                src_ref=ref, dst_ref=ref, send_sem=fin_s.at[which, i], recv_sem=fin_r.at[which, i],
                device_id=core_pair, device_id_type=MESH,
            ).wait_recv()

        @pl.loop(0, 8)
        def _(k):
            for n, (dx, dz) in enumerate(offsets):
                chip = (k // 2) * 2 + (k % 2 + dz) % 2
                cols = pl.ds(pl.multiple_of((fsdp_slot(dx, dz) * 8 + chip) * 128, 128), 128)
                part = slice(n * 64, (n + 1) * 64)
                both = jnp.concatenate([got[which, k * 2, :, part], got[which, k * 2 + 1, :, part]], axis=1)
                out_ref[:, cols] = (both.astype(F32) * os_ref[:, cols]).astype(BF16)

    collect(0, ((0, 0), (1, 0), (3, 0), (0, 1)))
    collect(1, ((2, 0), (1, 1), (3, 1), (2, 1)))

    @pl.loop(1, 16)
    def _(i):
        block_copy(i).wait_send()
        final_copy(0, i).wait_send()
        final_copy(1, i).wait_send()

    len_copy.wait_send()
    att_copy(0).wait_send()
    att_copy(1).wait_send()
    for n in range(2):
        core_copy(n, c).wait_send()
        row_copy(n, y * 2 + 1 - zl).wait_send()
    for group in (out_gather, one_gather, two_gather, row_gather, row_across, *att_gathers, *att_acrosses):
        group.sent()


def shards(
    hidden_in, lengths, norm_gain, query_weight, key_weight, value_weight, out_weight,
    query_scale, key_scale, value_scale, out_scale,
):
    vmem = pl.BlockSpec(memory_space=pltpu.VMEM)
    any_space = pl.BlockSpec(memory_space=pl.ANY)
    smem = pl.BlockSpec(memory_space=pltpu.SMEM)
    dma = pltpu.SemaphoreType.DMA
    return pl.pallas_call(
        kernel,
        out_shape=jax.ShapeDtypeStruct((32, D), BF16),
        in_specs=[any_space, smem, vmem, any_space, any_space, any_space, any_space, vmem, vmem, vmem, vmem],
        out_specs=vmem,
        scratch_shapes=[
            pltpu.VMEM((2, 8, TOK, 1024), BF16),
            pltpu.VMEM((64, D), BF16),
            pltpu.VMEM((64, 1024), BF16),
            pltpu.VMEM((64, 1024), BF16),
            pltpu.VMEM((64, D), BF16),
            pltpu.VMEM((16, 64, 640), BF16),
            pltpu.VMEM((1024, 640), BF16),
            pltpu.VMEM((8, 1024, 256), BF16),
            pltpu.VMEM((8, 1024, 128), BF16),
            pltpu.VMEM((8, 64, D), BF16),
            pltpu.VMEM((2, 8, 128), jnp.int32),
            pltpu.VMEM((2, TOK, 256), F32),
            pltpu.VMEM((2, TOK, 256), F32),
            pltpu.VMEM((2, TOK, HD), F32),
            pltpu.VMEM((2, TOK, HD), F32),
            pltpu.VMEM((2, TOK, HD), F32),
            pltpu.VMEM((2, TOK, HD), jnp.int32),
            pltpu.VMEM((2, 2, TOK, HD), BF16),
            pltpu.VMEM((2, 2, TOK, HD), BF16),
            pltpu.VMEM((2, TOK, HD), BF16),
            pltpu.VMEM((8, TOK, 1024), BF16),
            pltpu.VMEM((2, TOK, 256), F32),
            pltpu.VMEM((2, TOK, 256), BF16),
            pltpu.VMEM((2, 16, 32, 256), BF16),
            dma((12,)), dma((16,)), dma((16,)), dma((3,)), dma((3,)), dma((2,)), dma((2,)), dma((2,)), dma((2,)),
            dma((2, 8)), dma((2, 8)), dma((2, 8)), dma((2, 8)),
            dma((2, 8)), dma((2, 8)), dma((2, 8)), dma((2, 8)), dma((4, 8)), dma((4, 8)),
            dma((2, 2, 8)), dma((2, 2, 8)), dma((2, 2, 8)), dma((2, 2, 8)),
            dma((2, 16)), dma((2, 16)),
        ],
        compiler_params=pltpu.CompilerParams(
            collective_id=0, has_side_effects=True, vmem_limit_bytes=60 * 1024 * 1024
        ),
        cost_estimate=pl.CostEstimate(flops=10_000_000_000, bytes_accessed=16_000_000, transcendentals=1_000_000),
        name="refresh_and_prefill",
    )(
        hidden_in, lengths, norm_gain.reshape(1, -1), query_weight, key_weight, value_weight, out_weight.T,
        query_scale.reshape(1, -1), key_scale.reshape(1, -1), value_scale.reshape(1, -1), out_scale.reshape(1, -1),
    )


def solution(mesh):
    in_specs = (
        P("fsdp", None),
        P("fsdp", None),
        P(),
        P(("fsdp", "tp"), None),
        P(("fsdp", "tp"), None),
        P(("fsdp", "tp"), None),
        P(None, ("fsdp", "tp")),
        P(),
        P(),
        P(),
        P(),
    )
    return jax.shard_map(
        shards, mesh=mesh, in_specs=in_specs, out_specs=P(("fsdp", "tp"), None), check_vma=False
    )
```

```python
import math

import jax
import jax.numpy as jnp
from jax import lax
from jax.experimental import pallas as pl
from jax.experimental.pallas import tpu as pltpu
from jax.sharding import PartitionSpec as P

MESH = pl.DeviceIdType.MESH
F32 = jnp.float32
BF16 = jnp.bfloat16

HD = 128
TOK = 512
D = 8192
SATURATE = 448.0
EPSILON = 1e-06
ROPE_BASE = 1000000.0
MASKED_SCORE = -1e30

OUT_TREE = {
    (1, 0): (0, 0, 1),
    (3, 0): (0, 0, -1),
    (0, 1): (0, 0, 0),
    (2, 0): (1, 0, 1),
    (2, 1): (2, 0, 0),
    (1, 1): (0, 1, 1),
    (3, 1): (0, 1, -1),
}
PAIR_TREE = {**OUT_TREE, (3, 1): (3, 0, 0)}
IN_TREE = {**OUT_TREE, (2, 1): (1, 1, 1)}


class Gather:
    def __init__(self, trees, slot, piece, send_sem, recv_sem, plus, minus, pair, source=None):
        self.trees, self.slot, self.piece = trees, slot, piece
        self.send_sem, self.recv_sem = send_sem, recv_sem
        self.to = {1: plus, -1: minus, 0: pair}
        self.source = source

    def index(self, u, dz, h):
        return self.slot((4 - u) % 4 if h % 2 else u, dz)

    def ref(self, u, dz, h):
        return self.piece(self.index(u, dz, h), h)

    def copy(self, u, dz, h):
        su, sdz, step = self.trees[h][(u, dz)]
        here = there = self.ref(su, sdz, h)
        if self.source is not None and (su, sdz) == (0, 0):
            here = self.source(h, step)
        return pltpu.make_async_remote_copy(
            src_ref=here,
            dst_ref=there,
            send_sem=self.send_sem.at[h, u * 2 + dz],
            recv_sem=self.recv_sem.at[h, u * 2 + dz],
            device_id=self.to[-step if h % 2 else step],
            device_id_type=MESH,
        )

    def send(self, h, *targets):
        for u, dz in targets:
            self.copy(u, dz, h).start()

    def pass_on(self, u, dz, h):
        self.send(h, *[to for to, by in self.trees[h].items() if by[:2] == (u, dz)])

    def arrived(self, u, dz, h):
        ref = self.ref(u, dz, h)
        pltpu.make_async_remote_copy(
            src_ref=ref,
            dst_ref=ref,
            send_sem=self.send_sem.at[h, u * 2 + dz],
            recv_sem=self.recv_sem.at[h, u * 2 + dz],
            device_id=self.to[1],
            device_id_type=MESH,
        ).wait_recv()

    def sent(self):
        for h, tree in enumerate(self.trees):
            for u, dz in tree:
                self.copy(u, dz, h).wait_send()


class Across:
    def __init__(self, gather, piece, send_sem, recv_sem, core_pair):
        self.gather, self.piece = gather, piece
        self.send_sem, self.recv_sem, self.core_pair = send_sem, recv_sem, core_pair
        self.keys = [(0, 0), *OUT_TREE]

    def copy(self, u, dz, h, other):
        ref = self.piece(self.gather.index(u, dz, h), h, other)
        return pltpu.make_async_remote_copy(
            src_ref=ref, dst_ref=ref, send_sem=self.send_sem.at[h, u * 2 + dz], recv_sem=self.recv_sem.at[h, u * 2 + dz],
            device_id=self.core_pair, device_id_type=MESH,
        )

    def send(self, u, dz, h):
        self.copy(u, dz, h, False).start()

    def arrived(self, u, dz, h):
        self.copy(u, dz, h, True).wait_recv()

    def sent(self):
        for h in range(2):
            for u, dz in self.keys:
                self.copy(u, dz, h, False).wait_send()


def choose(i, values):
    result = values[-1]
    for n in range(len(values) - 2, -1, -1):
        result = jnp.where(i == n, values[n], result)
    return result


def kernel(
    hidden_ref, lengths_ref, gain_ref, wq_ref, wk_ref, wv_ref, wo_ref, qs_ref, ks_ref, vs_ref, os_ref,
    out_ref,
    nrm, raw_q, raw_k, raw_v, raw_o, snd, w_own, w_one, w_two, wo, len_t, acc_a, acc_b, acc_c, cos_t, sin_t, begin_t,
    q_t, kv_t, att_out, att, acc_o, ost, got,
    load_sem, a2a_s, a2a_r, one_s, one_r, core_s, core_r, rows_s, rows_r, ring_s, ring_r, racross_s, racross_r,
    one_in_s, one_in_r, two_in_s, two_in_r, o_s, o_r, att_s, att_r, across_s, across_r, fin_s, fin_r,
):
    f = lax.axis_index("fsdp")
    t = lax.axis_index("tp")
    x, zh = f // 2, f % 2
    y, zl, c = t // 4, (t // 2) % 2, t % 2
    rz = (zl + zh) % 2
    role = y * 2 + rz
    hb = role * 2 + c

    def device(ff, tt):
        return {"fsdp": ff, "tp": tt}

    x_plus = device(((x + 1) % 4) * 2 + zh, t)
    x_minus = device(((x + 3) % 4) * 2 + zh, t)
    z_pair = device(x * 2 + 1 - zh, y * 4 + (1 - zl) * 2 + c)
    y_plus = device(f, ((y + 1) % 4) * 4 + zl * 2 + c)
    y_minus = device(f, ((y + 3) % 4) * 4 + zl * 2 + c)
    zl_pair = device(f, y * 4 + (1 - zl) * 2 + c)
    core_pair = device(f, y * 4 + zl * 2 + 1 - c)

    barrier = pltpu.get_barrier_semaphore()
    for other in (x_plus, x_minus, z_pair):
        pl.semaphore_signal(barrier, inc=1, device_id=other, device_id_type=MESH)

    @pl.loop(1, 16)
    def _(i):
        pl.semaphore_signal(barrier, inc=1, device_id=device(f, (t + i) % 16), device_id_type=MESH)

    loads = [
        pltpu.make_async_copy(src, dst, load_sem.at[n])
        for n, (src, dst) in enumerate([(wo_ref, raw_o), (wq_ref, raw_q), (wk_ref, raw_k), (wv_ref, raw_v)])
    ]
    for j in range(8):
        loads.append(pltpu.make_async_copy(hidden_ref.at[:, pl.ds(j * 1024, 1024)], nrm.at[0, j], load_sem.at[4 + j]))
    for load in loads:
        load.start()

    def quantize(weight, inverse):
        return jnp.clip(weight.astype(F32) * inverse, -SATURATE, SATURATE).astype(BF16)

    def fsdp_slot(dx, dz):
        return ((x + 4 - dx) % 4) * 2 + (zh + dz) % 2

    out_gather = Gather(
        [OUT_TREE] * 4, fsdp_slot, lambda s, h: wo.at[s, pl.ds(h * 16, 16)], o_s, o_r,
        x_plus, x_minus, z_pair,
    )
    one_gather = Gather(
        [IN_TREE] * 2, fsdp_slot, lambda s, h: w_one.at[s, pl.ds(h * 512, 512)], one_in_s, one_in_r, x_plus, x_minus, z_pair,
        lambda h, step: w_own.at[pl.ds(h * 512, 512), pl.ds(128 if step else 256, 256)],
    )
    two_gather = Gather(
        [IN_TREE] * 2, fsdp_slot, lambda s, h: w_two.at[s, pl.ds(h * 512, 512)], two_in_s, two_in_r, x_plus, x_minus, z_pair,
        lambda h, step: w_own.at[pl.ds(h * 512, 512), pl.ds(0 if step else 512, 128)],
    )
    def chip_slot(dy, dz):
        return ((y + 4 - dy) % 4) * 2 + (zl + dz) % 2

    def row_piece(s, h, core):
        return nrm.at[1, s, pl.ds(h * 256, 256), pl.ds(pl.multiple_of(core * 512, 512), 512)]

    row_gather = Gather(
        [OUT_TREE] * 2, chip_slot, lambda s, h: row_piece(s, h, c), ring_s, ring_r, y_plus, y_minus, zl_pair
    )
    row_across = Across(
        row_gather, lambda s, h, other: row_piece(s, h, 1 - c if other else c), racross_s, racross_r, core_pair
    )
    def att_slot(dy, dz):
        return ((y + 4 - dy) % 4) * 2 + (rz + dz) % 2

    def att_piece(s, core, half, n):
        return att.at[s, :, pl.ds(pl.multiple_of(core * 512 + half * 256 + n * 128, 128), 128)]

    att_gathers = [
        Gather(
            [OUT_TREE] * 2, att_slot, lambda s, h, n=n: att_piece(s, c, (zh + h) % 2, n),
            att_s.at[n], att_r.at[n], y_plus, y_minus, zl_pair,
        )
        for n in range(2)
    ]
    att_acrosses = [
        Across(
            att_gathers[n], lambda s, h, other, n=n: att_piece(s, 1 - c if other else c, (zh + h) % 2, n),
            across_s.at[n], across_r.at[n], core_pair,
        )
        for n in range(2)
    ]

    loads[0].wait()
    chip_cols = pl.ds(pl.multiple_of((f * 8 + t // 2) * 128, 128), 128)
    chip_scale = jnp.broadcast_to(1.0 / os_ref[:, chip_cols], (128, 128))
    on_diagonal = lax.broadcasted_iota(jnp.int32, (128, 128), 0) == lax.broadcasted_iota(jnp.int32, (128, 128), 1)
    chip_column = jnp.sum(jnp.where(on_diagonal, chip_scale, 0.0), axis=1, keepdims=True)
    own_scale = jnp.where(c == 0, chip_column[:64], chip_column[64:])

    @pl.loop(0, 16)
    def _(i):
        cols = pl.ds(pl.multiple_of(i * 512, 512), 512)
        wo[f, :, cols] = quantize(raw_o[:, cols], own_scale)

    pl.semaphore_wait(barrier, 18)
    for place in ((1, 0), (3, 0)):
        for h in range(4):
            out_gather.send(h, place)
    out_gather.send(0, (0, 1))

    for load in loads[1:4]:
        load.wait()

    @pl.loop(0, 8)
    def _(r):
        for n in range(2):
            for part, head, place in ((zh, 1, 0), (zh, 0, 128), (1 - zh, 0, 384), (1 - zh, 1, 512)):
                cols = pl.ds(pl.multiple_of((r * 2 + n) * 512 + part * 256 + head * 128, 128), 128)
                snd[r * 2 + n, :, place:place + 128] = quantize(raw_q[:, cols], 1.0 / qs_ref[:, cols])
        cols = pl.ds(pl.multiple_of(r * 128, 128), 128)
        snd[r * 2, :, 256:384] = quantize(raw_k[:, cols], 1.0 / ks_ref[:, cols])
        snd[r * 2 + 1, :, 256:384] = quantize(raw_v[:, cols], 1.0 / vs_ref[:, cols])

    for n in range(8):
        len_t[0, n:n + 1, :] = jnp.full((1, 128), lengths_ref[0, n], jnp.int32)

    def block_copy(i):
        to = (t + i) % 16
        block = ((to // 4) * 2 + ((to // 2) % 2 + zh) % 2) * 2 + to % 2
        return pltpu.make_async_remote_copy(
            src_ref=snd.at[block],
            dst_ref=w_own.at[pl.ds(pl.multiple_of(t * 64, 64), 64)],
            send_sem=a2a_s.at[i],
            recv_sem=a2a_r.at[i],
            device_id=device(f, to),
            device_id_type=MESH,
        )

    @pl.loop(1, 16)
    def _(i):
        block_copy(i).start()

    w_own[pl.ds(pl.multiple_of(t * 64, 64), 64)] = snd[hb]

    def one_copy(n, src, dst, device_id):
        return pltpu.make_async_remote_copy(
            src_ref=src, dst_ref=dst, send_sem=one_s.at[n], recv_sem=one_r.at[n],
            device_id=device_id, device_id_type=MESH,
        )

    len_copy = one_copy(0, len_t.at[0], len_t.at[1], z_pair)
    len_copy.start()

    for load in loads[4:]:
        load.wait()

    def row_copy(h, chip):
        rows, cols = pl.ds(h * 256, 256), pl.ds(pl.multiple_of(c * 512, 512), 512)
        return pltpu.make_async_remote_copy(
            src_ref=nrm.at[0, chip, rows, cols], dst_ref=nrm.at[1, chip, rows, cols],
            send_sem=rows_s.at[h], recv_sem=rows_r.at[h], device_id=z_pair, device_id_type=MESH,
        )

    for h in range(2):
        @pl.loop(h * 16, h * 16 + 16)
        def _(i):
            rows = pl.ds(pl.multiple_of(i * 16, 16), 16)
            square = jnp.zeros((16, 1024), F32)
            for j in range(8):
                wide = nrm[0, j, rows, :].astype(F32)
                square += wide * wide
            inverse = lax.rsqrt(jnp.sum(square, axis=1, keepdims=True) * (1.0 / D) + EPSILON)
            for j in range(8):
                wide = nrm[0, j, rows, :].astype(F32)
                nrm[0, j, rows, :] = (wide * inverse * gain_ref[:, j * 1024:(j + 1) * 1024]).astype(BF16)

        row_copy(h, y * 2 + 1 - zl).start()

    place = lax.broadcasted_iota(jnp.int32, (TOK, 128), 0)
    lane = lax.broadcasted_iota(jnp.int32, (TOK, 128), 1)

    def tables(replica):
        begin = jnp.zeros((TOK, 128), jnp.int32)
        start = jnp.zeros((1, 128), jnp.int32)
        for n in range(8):
            begin = jnp.where(place >= start, start, begin)
            start = start + len_t[replica, n:n + 1, :]
        begin_t[replica] = begin
        frequency = jnp.exp((lane % 64).astype(F32) * (-2.0 * math.log(ROPE_BASE) / HD))
        angle = (place - begin).astype(F32) * frequency
        cos_t[replica] = jnp.cos(angle)
        sine = jnp.sin(angle)
        sin_t[replica] = jnp.where(lane < 64, -sine, sine)

    tables(0)
    len_copy.wait_recv()
    tables(1)

    def row_take(h):
        row_copy(h, y * 2 + zl).wait_recv()
        row_gather.send(h, (1, 0), (0, 1))
        row_across.send(0, 0, h)

    def row_wait(u, dz):
        for h in range(2):
            row_gather.arrived(u, dz, h)
            row_gather.pass_on(u, dz, h)
            row_across.send(u, dz, h)

    row_take(0)

    for h in range(2):
        @pl.loop(h * 8, h * 8 + 8)
        def _(src):
            @pl.when(src != t)
            def _():
                ref = w_own.at[pl.ds(pl.multiple_of(src * 64, 64), 64)]
                i = (t + 16 - src) % 16
                pltpu.make_async_remote_copy(
                    src_ref=ref, dst_ref=ref, send_sem=a2a_s.at[i], recv_sem=a2a_r.at[i],
                    device_id=core_pair, device_id_type=MESH,
                ).wait_recv()

    def open_with(gather, *places):
        for place in places:
            for h in range(2):
                gather.send(h, place)

    open_with(one_gather, (1, 0), (0, 1), (3, 0))
    open_with(two_gather, (0, 1))
    for h in range(1, 4):
        out_gather.send(h, (0, 1))
    row_take(1)
    open_with(row_gather, (3, 0))

    for total in (acc_a, acc_b, acc_c, acc_o):
        total[...] = jnp.zeros_like(total)

    def project(gather, replica, places):
        for dz in range(2):
            some = [(u, h) for u, z in places for h in range(2) if z == dz and (u, z) != (0, 0)]
            if not some:
                continue
            slots, halves = [gather.index(u, dz, h) for u, h in some], [h for _, h in some]
            weight, total = (w_one, (acc_a, acc_b)[dz]) if gather is one_gather else (w_two, acc_c)

            @pl.loop(0, len(some))
            def _(i):
                s, h = choose(i, slots), choose(i, halves)
                cols = pl.ds(pl.multiple_of(h * 512, 512), 512)
                total[replica] += jnp.dot(nrm[replica, s, :, cols], weight[s, cols, :], preferred_element_type=F32)

        if (0, 0) in places:
            lanes, total = (slice(128, 384), acc_a) if gather is one_gather else (slice(0, 128), acc_c)

            @pl.loop(0, 2)
            def _(h):
                cols = pl.ds(pl.multiple_of(h * 512, 512), 512)
                total[replica] += jnp.dot(nrm[replica, f, :, cols], w_own[cols, lanes], preferred_element_type=F32)

    def project_items(gather, replicas, places):
        first = gather is one_gather
        for dz in range(2):
            slots = [fsdp_slot(u, z) for u, z in places if z == dz and (u, z) != (0, 0)]
            if not slots:
                continue
            weight, total = (w_one, (acc_a, acc_b)[dz]) if first else (w_two, acc_c)

            @pl.loop(0, len(slots) * len(replicas))
            def _(i):
                s = choose(i % len(slots), slots)
                replica = choose(i // len(slots), replicas)
                total[replica] += jnp.dot(nrm[replica, s], weight[s], preferred_element_type=F32)

        if (0, 0) in places:
            lanes, total = (slice(128, 384), acc_a) if first else (slice(0, 128), acc_c)

            @pl.loop(0, len(replicas))
            def _(i):
                replica = choose(i, replicas)
                total[replica] += jnp.dot(nrm[replica, f], w_own[:, lanes], preferred_element_type=F32)

    def wait(gather, *places):
        for u, dz in places:
            for h in range(len(gather.trees)):
                gather.arrived(u, dz, h)

    def relay(gather, u, dz):
        for h in range(len(gather.trees)):
            gather.arrived(u, dz, h)
            if dz == 0:
                gather.pass_on(u, dz, h)
        if dz == 1 and u == 0:
            for place in ((1, 1), (3, 1)):
                for h, tree in enumerate(gather.trees):
                    if tree[place][:2] == (0, 1):
                        gather.send(h, place)
        elif dz == 1:
            for h in range(len(gather.trees)):
                gather.pass_on(u, dz, h)

    def out_relay(u, dz, *parts):
        for h in parts:
            out_gather.arrived(u, dz, h)
            out_gather.pass_on(u, dz, h)

    project(one_gather, 0, [(0, 0)])
    project_items(two_gather, (0,), [(0, 0)])
    row_wait(1, 0)
    relay(one_gather, 1, 0)
    project(one_gather, 0, [(1, 0)])
    row_wait(0, 1)
    relay(one_gather, 0, 1)
    wait(one_gather, (3, 0))
    project(one_gather, 0, [(0, 1), (3, 0)])
    row_wait(3, 0)
    row_wait(2, 0)
    wait(one_gather, (2, 0))
    project(one_gather, 0, [(2, 0)])
    relay(one_gather, 1, 1)
    out_relay(1, 0, 0, 1)
    for h in range(4):
        out_gather.arrived(3, 0, h)
    out_gather.pass_on(3, 0, 2)
    project(one_gather, 0, [(1, 1)])
    row_wait(1, 1)
    wait(one_gather, (3, 1))
    open_with(two_gather, (1, 0), (3, 0))
    relay(two_gather, 0, 1)
    project(one_gather, 0, [(3, 1)])
    project_items(two_gather, (0,), [(0, 1)])
    row_wait(3, 1)
    row_wait(2, 1)
    for h in range(2):
        for u in range(4):
            for dz in range(2):
                row_across.arrived(u, dz, h)
    project_items(one_gather, (1,), [(0, 0), (1, 0), (3, 0), (2, 0), (0, 1), (1, 1), (3, 1)])
    wait(one_gather, (2, 1))
    project_items(one_gather, (1, 0), [(2, 1)])

    def rope(v, replica):
        return v * cos_t[replica] + pltpu.roll(v, 64, axis=1) * sin_t[replica]

    def core_copy(replica, core):
        return pltpu.make_async_remote_copy(
            src_ref=kv_t.at[replica, core], dst_ref=kv_t.at[replica, core],
            send_sem=core_s.at[replica], recv_sem=core_r.at[replica],
            device_id=core_pair, device_id_type=MESH,
        )

    kv_cols = pl.ds(pl.multiple_of(role * 128, 128), 128)
    for replica in (1, 0):
        product = acc_a[replica, :, 128:256] + acc_b[replica, :, 0:128]
        key_raw = (product * ks_ref[:, kv_cols]).astype(BF16).astype(F32)
        value = product * vs_ref[:, kv_cols]
        kv_t[replica, c] = jnp.where(c == 0, rope(key_raw, replica), value).astype(BF16)
        core_copy(replica, c).start()

    def query(replica, n):
        product = acc_c[replica] if n else acc_a[replica, :, 0:128] + acc_b[replica, :, 128:256]
        scale = qs_ref[:, pl.ds(pl.multiple_of(hb * 512 + zh * 256 + n * 128, 128), 128)]
        q_t[replica, n] = rope(product * scale, replica).astype(BF16)

    def attend(replica, n, out):
        query(replica, n)
        for b in range(4):
            first = max(0, b * 128 - 256)
            width = (b + 1) * 128 - first
            rows = slice(b * 128, (b + 1) * 128)
            keys = slice(first, first + width)
            scores = lax.dot_general(
                q_t[replica, n, rows], kv_t[replica, 0, keys], (((1,), (1,)), ((), ())), preferred_element_type=F32
            ) * HD ** (-0.5)
            p = lax.broadcasted_iota(jnp.int32, (128, width), 0) + b * 128
            s = lax.broadcasted_iota(jnp.int32, (128, width), 1) + first
            keep = (s <= p) & (s >= begin_t[replica, rows, 0:1])
            scores = jnp.where(keep, scores, MASKED_SCORE)
            weights = jnp.exp(scores - jnp.max(scores, axis=1, keepdims=True))
            total = jnp.sum(weights, axis=1, keepdims=True)
            mixed = jnp.dot(weights.astype(BF16), kv_t[replica, 1, keys], preferred_element_type=F32)
            out[rows, :] = (mixed / total).astype(BF16)

    def att_copy(n):
        return one_copy(1 + n, att_out.at[n], att_piece(role, c, zh, n), z_pair)

    def att_arrived(n):
        one_copy(1 + n, att_out.at[n], att_piece(role, c, 1 - zh, n), z_pair).wait_recv()
        att_gathers[n].pass_on(0, 0, 1)
        att_acrosses[n].send(0, 0, 1)

    def att_own(n):
        attend(0, n, att_piece(role, c, zh, n))
        att_gathers[n].pass_on(0, 0, 0)
        att_acrosses[n].send(0, 0, 0)

    def take(n, *places):
        for u, dz in places:
            for h in range(2):
                att_gathers[n].arrived(u, dz, h)
                att_gathers[n].pass_on(u, dz, h)
                att_acrosses[n].send(u, dz, h)

    early = [fsdp_slot(dx, dz) for dx, dz in ((0, 0), (1, 0), (3, 0), (0, 1))]
    late = [fsdp_slot(dx, dz) for dx, dz in ((2, 0), (1, 1), (3, 1), (2, 1))]

    def mix_head(n, *places):
        for u, dz in places:
            for h in range(2):
                att_acrosses[n].arrived(u, dz, h)
        roles = [att_slot(u, dz) for u, dz in places]

        @pl.loop(0, len(roles))
        def _(i):
            r = choose(i, roles)
            left = jnp.concatenate([att[r, :, k * 256 + n * 128:k * 256 + n * 128 + 128] for k in range(4)], axis=1)
            cols = [pl.ds(pl.multiple_of(r * 1024 + k * 256 + n * 128, 128), 128) for k in range(4)]
            right = jnp.concatenate(
                [jnp.concatenate([wo[s, :, k] for k in cols], axis=1) for s in early], axis=0
            )
            acc_o[0] += lax.dot_general(left, right, (((1,), (1,)), ((), ())), preferred_element_type=F32)

    def mix_late():
        @pl.loop(0, 8)
        def _(r):
            cols = pl.ds(pl.multiple_of(r * 1024, 1024), 1024)
            right = jnp.concatenate([wo[s, :, cols] for s in late], axis=0)
            acc_o[1] += lax.dot_general(att[r], right, (((1,), (1,)), ((), ())), preferred_element_type=F32)

    ring = [(0, 0), (1, 0), (3, 0), (2, 0)]
    beyond = [(0, 1), (1, 1), (3, 1), (2, 1)]
    core_copy(1, 1 - c).wait_recv()
    attend(1, 0, att_out.at[0])
    att_copy(0).start()
    out_gather.pass_on(3, 0, 3)
    core_copy(0, 1 - c).wait_recv()
    att_own(0)
    att_arrived(0)
    relay(two_gather, 1, 0)
    out_relay(2, 0, 0, 1)
    take(0, (1, 0), (0, 1))
    relay(two_gather, 1, 1)
    out_relay(1, 0, 2, 3)
    relay(out_gather, 0, 1)
    project_items(two_gather, (1,), [(0, 0), (0, 1)])
    take(0, (3, 0), (2, 0))
    wait(two_gather, (3, 0), (2, 0), (3, 1))
    project_items(two_gather, (1, 0), [(1, 0), (3, 0), (2, 0), (1, 1), (3, 1)])
    take(0, (1, 1), (3, 1), (2, 1))
    wait(two_gather, (2, 1))
    project_items(two_gather, (1, 0), [(2, 1)])
    attend(1, 1, att_out.at[1])
    att_copy(1).start()
    att_own(1)
    mix_head(0, *ring)
    att_arrived(1)

    def finish(which):
        ost[which] = acc_o[which].astype(BF16)

        @pl.loop(1, 16)
        def _(i):
            final_copy(which, i).start()

        got[which, t] = ost[which, pl.ds(pl.multiple_of(t * 32, 32), 32)]

    def final_copy(which, i):
        to = (t + i) % 16
        return pltpu.make_async_remote_copy(
            src_ref=ost.at[which, pl.ds(pl.multiple_of(to * 32, 32), 32)],
            dst_ref=got.at[which, t],
            send_sem=fin_s.at[which, i],
            recv_sem=fin_r.at[which, i],
            device_id=device(f, to),
            device_id_type=MESH,
        )

    take(1, (1, 0), (0, 1))
    out_relay(2, 0, 2, 3)
    mix_head(0, *beyond)
    take(1, (3, 0), (2, 0))
    mix_head(1, *ring)
    take(1, (1, 1), (3, 1), (2, 1))
    mix_head(1, *beyond)
    finish(0)
    wait(out_gather, (1, 1), (3, 1), (2, 1))
    mix_late()
    finish(1)

    def collect(which, offsets):
        @pl.loop(1, 16)
        def _(i):
            ref = got.at[which, (t + 16 - i) % 16]
            pltpu.make_async_remote_copy(
                src_ref=ref, dst_ref=ref, send_sem=fin_s.at[which, i], recv_sem=fin_r.at[which, i],
                device_id=core_pair, device_id_type=MESH,
            ).wait_recv()

        @pl.loop(0, 8)
        def _(k):
            for n, (dx, dz) in enumerate(offsets):
                chip = (k // 2) * 2 + (k % 2 + dz) % 2
                cols = pl.ds(pl.multiple_of((fsdp_slot(dx, dz) * 8 + chip) * 128, 128), 128)
                part = slice(n * 64, (n + 1) * 64)
                both = jnp.concatenate([got[which, k * 2, :, part], got[which, k * 2 + 1, :, part]], axis=1)
                out_ref[:, cols] = (both.astype(F32) * os_ref[:, cols]).astype(BF16)

    collect(0, ((0, 0), (1, 0), (3, 0), (0, 1)))
    collect(1, ((2, 0), (1, 1), (3, 1), (2, 1)))

    @pl.loop(1, 16)
    def _(i):
        block_copy(i).wait_send()
        final_copy(0, i).wait_send()
        final_copy(1, i).wait_send()

    len_copy.wait_send()
    att_copy(0).wait_send()
    att_copy(1).wait_send()
    for n in range(2):
        core_copy(n, c).wait_send()
        row_copy(n, y * 2 + 1 - zl).wait_send()
    for group in (out_gather, one_gather, two_gather, row_gather, row_across, *att_gathers, *att_acrosses):
        group.sent()


def shards(
    hidden_in, lengths, norm_gain, query_weight, key_weight, value_weight, out_weight,
    query_scale, key_scale, value_scale, out_scale,
):
    vmem = pl.BlockSpec(memory_space=pltpu.VMEM)
    any_space = pl.BlockSpec(memory_space=pl.ANY)
    smem = pl.BlockSpec(memory_space=pltpu.SMEM)
    dma = pltpu.SemaphoreType.DMA
    return pl.pallas_call(
        kernel,
        out_shape=jax.ShapeDtypeStruct((32, D), BF16),
        in_specs=[any_space, smem, vmem, any_space, any_space, any_space, any_space, vmem, vmem, vmem, vmem],
        out_specs=vmem,
        scratch_shapes=[
            pltpu.VMEM((2, 8, TOK, 1024), BF16),
            pltpu.VMEM((64, D), BF16),
            pltpu.VMEM((64, 1024), BF16),
            pltpu.VMEM((64, 1024), BF16),
            pltpu.VMEM((64, D), BF16),
            pltpu.VMEM((16, 64, 640), BF16),
            pltpu.VMEM((1024, 640), BF16),
            pltpu.VMEM((8, 1024, 256), BF16),
            pltpu.VMEM((8, 1024, 128), BF16),
            pltpu.VMEM((8, 64, D), BF16),
            pltpu.VMEM((2, 8, 128), jnp.int32),
            pltpu.VMEM((2, TOK, 256), F32),
            pltpu.VMEM((2, TOK, 256), F32),
            pltpu.VMEM((2, TOK, HD), F32),
            pltpu.VMEM((2, TOK, HD), F32),
            pltpu.VMEM((2, TOK, HD), F32),
            pltpu.VMEM((2, TOK, HD), jnp.int32),
            pltpu.VMEM((2, 2, TOK, HD), BF16),
            pltpu.VMEM((2, 2, TOK, HD), BF16),
            pltpu.VMEM((2, TOK, HD), BF16),
            pltpu.VMEM((8, TOK, 1024), BF16),
            pltpu.VMEM((2, TOK, 256), F32),
            pltpu.VMEM((2, TOK, 256), BF16),
            pltpu.VMEM((2, 16, 32, 256), BF16),
            dma((12,)), dma((16,)), dma((16,)), dma((3,)), dma((3,)), dma((2,)), dma((2,)), dma((2,)), dma((2,)),
            dma((2, 8)), dma((2, 8)), dma((2, 8)), dma((2, 8)),
            dma((2, 8)), dma((2, 8)), dma((2, 8)), dma((2, 8)), dma((4, 8)), dma((4, 8)),
            dma((2, 2, 8)), dma((2, 2, 8)), dma((2, 2, 8)), dma((2, 2, 8)),
            dma((2, 16)), dma((2, 16)),
        ],
        compiler_params=pltpu.CompilerParams(
            collective_id=0, has_side_effects=True, vmem_limit_bytes=60 * 1024 * 1024
        ),
        cost_estimate=pl.CostEstimate(flops=10_000_000_000, bytes_accessed=16_000_000, transcendentals=1_000_000),
        name="refresh_and_prefill",
    )(
        hidden_in, lengths, norm_gain.reshape(1, -1), query_weight, key_weight, value_weight, out_weight.T,
        query_scale.reshape(1, -1), key_scale.reshape(1, -1), value_scale.reshape(1, -1), out_scale.reshape(1, -1),
    )


def solution(mesh):
    in_specs = (
        P("fsdp", None),
        P("fsdp", None),
        P(),
        P(("fsdp", "tp"), None),
        P(("fsdp", "tp"), None),
        P(("fsdp", "tp"), None),
        P(None, ("fsdp", "tp")),
        P(),
        P(),
        P(),
        P(),
    )
    return jax.shard_map(
        shards, mesh=mesh, in_specs=in_specs, out_specs=P(("fsdp", "tp"), None), check_vma=False
    )
```
